32 devices in a mesh: owner: 2 (over x), ctx: 16 (over z, y, core).
Axes of the slice: x: 2, y: 2, z: 4, core: 2. Of those that a mesh axis runs over, the one named last changes fastest.
Arguments:
- span_cache: bfloat16 [256, 128, 1024], P(('owner', 'ctx')), may hold values from -8 to 8
- retrieval: int32 [2, 128], P(None, 'ctx'), may hold values from 0 to 255, as said below
- counts: int32 [2], replicated, may hold values from 32 to 128, as said below
- recompute_pos: int32 [2, 128], P('owner'), may hold values from 0 to 1023, as said below
- hidden: bfloat16 [2, 128, 8192], P('owner', None, 'ctx'), may hold values from -6 to 6
- kv_weight: bfloat16 [8192, 1024], P('ctx'), may hold values from -0.0625 to 0.0625
- queries: bfloat16 [2, 128, 4096], P('owner', 'ctx'), may hold values from -8 to 8
- block_mask: int32 [2, 128, 128], P('owner', None, 'ctx'), may hold values from 0 to 1, as said below
Outputs:
- context_kv: bfloat16 [2, 16384, 1024], P('owner', 'ctx')
- attended: bfloat16 [2, 128, 4096], P('owner', 'ctx')
The draws below stay inside these ranges and needn't reach their ends.
Inputs may be any that keep to these rules, and one draw needn't show every extreme that they name: `retrieval`: the span for block b of a request is stored on index b // 8 of ctx of some owner group o: its number is (o * 16 + b // 8) * 8 + s. Among the 8 blocks of one request on one index of ctx at most 4 name spans of one owner group, and in every draw some reach 4. `counts`: some request uses all 128 blocks in every draw. `recompute_pos`: the 8 positions of one request on one index of ctx are distinct. `block_mask`: every query block may see itself and those of the first 4 blocks not after it; no block sees a later one.
All inputs are finite; a program needn't handle non-finite values.
Results may differ from the reference program's by a relative error of at most 0.023.
Values may be sent and summed in bfloat16 or wider, within the bound.
A program may use at most 128 MiB of HBM per device.

```python
import jax
import jax.numpy as jnp
from jax import lax

D = 8192
QH = 32
KVH = 4
HD = 128
BLK = 128
NBD = 8
RCP = 8
SLOTS = 8
CAP = 4
PREFIX = 4
CTX_DEV = 1024
NB = 128
SEQ = 16384
REQS = 2
SPANS = 256
NQ = 128
KVW = 1024
N_OWNER = 2
N_CTX = 16


def draw_span_cache(key, part):
    key_body = jax.random.fold_in(jax.random.fold_in(key, 11), 0)
    shape = (SPANS, BLK, 2 * KVH * HD)
    drawn = jnp.clip(jax.random.normal(key_body, shape, jnp.float32), -5.0, 5.0)
    return drawn.astype(jnp.bfloat16)


def draw_queries(key, part):
    key_body = jax.random.fold_in(jax.random.fold_in(key, 23), 0)
    shape = (REQS, NQ, QH * HD)
    drawn = jnp.clip(jax.random.normal(key_body, shape, jnp.float32), -5.0, 5.0)
    return drawn.astype(jnp.bfloat16)


def draw_retrieval(key, part):
    key_perm, key_jitter, key_slot, key_shuffle = jax.random.split(jax.random.fold_in(key, 31), 4)
    contender_total = N_OWNER * CAP
    heat_order = jax.random.permutation(key_perm, N_OWNER)
    demand_ordinal_position = jnp.zeros((N_OWNER,), jnp.int32).at[heat_order].set(jnp.arange(N_OWNER, dtype=jnp.int32))
    contender_holder_device = jnp.repeat(jnp.arange(N_OWNER, dtype=jnp.int32), CAP)
    stochastic_jitter = jax.random.randint(key_jitter, (REQS, N_CTX, contender_total), 0, 1024)
    demand_increment = (N_OWNER - demand_ordinal_position[contender_holder_device]) * 160
    mandated_selection = jnp.where((jnp.arange(N_CTX) == 0)[:, None] & (demand_ordinal_position[contender_holder_device] == 0)[None, :], 100000, 0)
    precedence_sequence = (stochastic_jitter + demand_increment[None, None, :] + mandated_selection[None, :, :]) * contender_total + jnp.arange(contender_total, dtype=jnp.int32)
    picked = jnp.argsort(-precedence_sequence, axis=-1)[..., :NBD]
    owners_drawn = contender_holder_device[picked]
    shuffle_keys = jax.random.randint(key_shuffle, (REQS, N_CTX, NBD), 0, 1 << 20) * NBD + jnp.arange(NBD, dtype=jnp.int32)
    shuffle = jnp.argsort(shuffle_keys, axis=-1)
    owners_drawn = jnp.take_along_axis(owners_drawn, shuffle, axis=-1)
    slot_draw = jax.random.randint(key_slot, (REQS, N_CTX, NBD), 0, SLOTS)
    span_ids = (owners_drawn * N_CTX + jnp.arange(N_CTX, dtype=jnp.int32)[None, :, None]) * SLOTS + slot_draw
    return span_ids.reshape(REQS, N_CTX * NBD).astype(jnp.int32)


def draw_counts(key, part):
    lower = max(PREFIX + 1, NB // 4)
    drawn = jax.random.randint(jax.random.fold_in(key, 41), (REQS,), lower, NB + 1)
    full_request = jax.random.randint(jax.random.fold_in(key, 43), (), 0, REQS)
    return jnp.where(jnp.arange(REQS) == full_request, NB, drawn).astype(jnp.int32)


def draw_recompute_pos(key, part):
    precedence_sequence = jax.random.randint(jax.random.fold_in(key, 53), (REQS, N_CTX, CTX_DEV), 0, 1 << 20) * CTX_DEV + jnp.arange(CTX_DEV, dtype=jnp.int32)
    picked = jnp.argsort(precedence_sequence, axis=-1)[..., :RCP]
    return picked.reshape(REQS, N_CTX * RCP).astype(jnp.int32)


def draw_block_mask(key, part):
    query_block = jnp.arange(NB, dtype=jnp.int32)[:, None]
    key_block = jnp.arange(NB, dtype=jnp.int32)[None, :]
    extra = jax.random.randint(jax.random.fold_in(key, 61), (REQS, NB, NB), 0, 8) == 0
    allowed = (key_block < PREFIX) | (key_block == query_block) | extra & (key_block < query_block)
    allowed = allowed & (key_block <= query_block)
    return allowed.astype(jnp.int32)


def steps_of(stream_key, dims, cuts, low, largest):
    level, own = 1.0, jax.random.fold_in(stream_key, 6)
    for dim, parts in cuts:
        heights = jnp.exp(jax.random.uniform(jax.random.fold_in(own, dim), (parts,), jnp.float32, low / len(cuts), largest / len(cuts)))
        level = level * jnp.repeat(heights, dims[dim] // parts).reshape([-1 if axis == dim else 1 for axis in range(len(dims))])
    return level


def centred(rng, shape, deviation, bound, pieces=(), held_as=jnp.bfloat16):
    entries = jax.random.normal(rng, shape, jnp.float32) * deviation
    if len(pieces) > 0:
        entries = steps_of(rng, shape, pieces, -0.22, 0.18) * entries
    return jnp.clip(entries, min=-bound, max=bound).astype(held_as)


def setup_inputs(seed: int = 0) -> dict:
    seeds = jax.random.split(jax.random.key(seed), 9)
    span_cache = draw_span_cache(jax.random.fold_in(seeds[8], 71), 0)
    retrieval = draw_retrieval(jax.random.fold_in(seeds[8], 71), 0)
    counts = draw_counts(jax.random.fold_in(seeds[8], 71), 0)
    recompute_pos = draw_recompute_pos(jax.random.fold_in(seeds[8], 71), 0)
    hidden = centred(seeds[4], (REQS, NQ, D), 1.0, 6.0, ((0, 2), (2, 16)))
    kv_weight = centred(seeds[5], (D, KVW), D ** -0.5, 0.0625, ((0, 16),))
    queries = draw_queries(jax.random.fold_in(seeds[8], 71), 0)
    block_mask = draw_block_mask(jax.random.fold_in(seeds[8], 71), 0)
    return dict(span_cache=span_cache, retrieval=retrieval, counts=counts, recompute_pos=recompute_pos, hidden=hidden, kv_weight=kv_weight, queries=queries, block_mask=block_mask)


def attend_request(query_rows, context_rows, query_pos, mask_rows, request_count):
    key_pos = jnp.arange(SEQ, dtype=jnp.int32)
    key_block = key_pos // BLK
    allowed = jnp.take(mask_rows, query_pos // BLK, axis=0)
    visible = jnp.repeat(allowed, BLK, axis=1) > 0
    visible = visible & (key_block[None, :] < request_count) & (key_pos[None, :] <= query_pos[:, None])
    key_rows = context_rows[:, :KVH * HD].astype(jnp.float32)
    value_rows = context_rows[:, KVH * HD:].astype(jnp.float32)
    query_float = query_rows.astype(jnp.float32)
    per_group = QH // KVH
    scaling = HD ** -0.5

    def one_head(head_index):
        kv_index = head_index // per_group
        query_head = lax.dynamic_slice_in_dim(query_float, head_index * HD, HD, 1)
        key_head = lax.dynamic_slice_in_dim(key_rows, kv_index * HD, HD, 1)
        value_head = lax.dynamic_slice_in_dim(value_rows, kv_index * HD, HD, 1)
        scores = jnp.dot(query_head, key_head.T, precision=lax.Precision.HIGHEST) * scaling
        scores = jnp.where(visible, scores, -1e30)
        highest = jnp.max(scores, axis=1, keepdims=True)
        weights = jnp.where(visible, jnp.exp(scores - highest), 0.0)
        weight_sum = jnp.sum(weights, axis=1, keepdims=True)
        rounded = lax.optimization_barrier(weights.astype(jnp.bfloat16)).astype(jnp.float32)
        numerator = jnp.dot(rounded, value_head, precision=lax.Precision.HIGHEST)
        return numerator / weight_sum

    per_head = lax.map(one_head, jnp.arange(QH, dtype=jnp.int32))
    return jnp.transpose(per_head, (1, 0, 2)).reshape(NQ, QH * HD).astype(jnp.bfloat16)


def reference(span_cache, retrieval, counts, recompute_pos, hidden, kv_weight, queries, block_mask):
    in_use = jnp.arange(NB, dtype=jnp.int32)[None, :] < counts[:, None]

    def build_request(request):
        span_ids = retrieval[request]
        blocks = jnp.take(span_cache, span_ids, axis=0)
        blocks = jnp.where(in_use[request][:, None, None], blocks, jnp.zeros_like(blocks))
        context_rows = blocks.reshape(SEQ, KVW)
        recomputed = jnp.dot(hidden[request], kv_weight, preferred_element_type=jnp.float32).astype(jnp.bfloat16)
        query_pos = (jnp.arange(NQ, dtype=jnp.int32) // RCP) * CTX_DEV + recompute_pos[request]
        context_rows = context_rows.at[query_pos].set(recomputed)
        attended = attend_request(queries[request], context_rows, query_pos, block_mask[request], counts[request])
        return context_rows, attended

    context_kv, attended = lax.map(build_request, jnp.arange(REQS, dtype=jnp.int32))
    return context_kv, attended
```

```python
import functools

import jax
import jax.numpy as jnp
from jax import lax
from jax.experimental import pallas as pl
from jax.experimental.pallas import tpu as pltpu
from jax.sharding import PartitionSpec as P

QH = 32
KVH = 4
HD = 128
BLK = 128
NBD = 8
RCP = 8
SLOTS = 8
CAP = 4
CTX_DEV = 1024
GROUP = QH // KVH
ROWS = GROUP * RCP
TILE = 4
STAT = 16
HIDDEN = -1e30
LOG2E = 1.4426950408889634
FACTOR = HD ** (-0.5) * LOG2E
MESH = pl.DeviceIdType.MESH


def kernel(
    owner_count,
    cycle_size,
    retrieval,
    counts,
    positions,
    position_col,
    mask_cols,
    hidden,
    weight,
    queries,
    spans,
    context,
    attended,
    x_send,
    slots,
    stage,
    every_query,
    red_send,
    red_recv,
    fresh,
    bias,
    values_ones,
    part_send,
    part_recv,
    levels,
    shares,
    x_sent,
    x_came,
    q_sent,
    q_came,
    r_sent,
    r_came,
    p_sent,
    p_came,
):
    me_o = lax.axis_index("owner")
    me = lax.axis_index("ctx")
    group_size = cycle_size * SLOTS
    f32, bf16 = jnp.float32, jnp.bfloat16

    barrier = pltpu.get_barrier_semaphore()

    @pl.loop(1, cycle_size)
    def _(step):
        peer = lax.rem(me + step, cycle_size)
        pl.semaphore_signal(barrier, inc=1, device_id={"ctx": peer}, device_id_type=MESH)

    @pl.loop(1, owner_count)
    def _(step):
        peer = lax.rem(me_o + step, owner_count)
        pl.semaphore_signal(barrier, inc=1, device_id={"owner": peer}, device_id_type=MESH)

    def chosen_slots(request):
        count = counts[request]
        rank = jnp.int32(0)
        chosen = [jnp.int32(0)] * CAP
        for b in range(NBD):
            span = retrieval[request, b]
            mine = (me * NBD + b < count) & (lax.div(span, group_size) == me_o)
            for k in range(CAP):
                chosen[k] = jnp.where(mine & (rank == k), lax.rem(span, SLOTS), chosen[k])
            rank = rank + jnp.where(mine, 1, 0)
        return chosen

    def pack(request, store):
        chosen = chosen_slots(request)
        for h in range(KVH):
            for k in range(CAP):
                for part in range(2):
                    column = (part * KVH + h) * HD
                    store(h, k, part, spans[chosen[k], :, column : column + HD])

    def x_copy(h, step):
        peer = lax.rem(me_o + step, owner_count)
        return pltpu.make_async_remote_copy(
            src_ref=x_send.at[h, peer],
            dst_ref=slots.at[h, pl.ds(me_o * CAP, CAP)],
            send_sem=x_sent.at[h, peer],
            recv_sem=x_came.at[h, me_o],
            device_id={"owner": peer},
            device_id_type=MESH,
        )

    @pl.loop(1, owner_count)
    def _(step):
        peer = lax.rem(me_o + step, owner_count)

        def store(h, k, part, block):
            x_send[h, peer, k, :, part * HD : (part + 1) * HD] = block

        pack(peer, store)

    pl.semaphore_wait(barrier, cycle_size + owner_count - 2)

    for h in range(KVH):

        @pl.loop(1, owner_count)
        def _(step):
            x_copy(h, step).start()

    def q_copy(h, peer):
        return pltpu.make_async_remote_copy(
            src_ref=queries.at[h],
            dst_ref=every_query.at[h, me],
            send_sem=q_sent.at[h, peer],
            recv_sem=q_came.at[h, me],
            device_id={"ctx": peer},
            device_id_type=MESH,
        )

    @pl.loop(0, me)
    def _(peer):
        q_copy(0, peer).start()

    partial = jnp.dot(hidden[...], weight[...], preferred_element_type=f32)
    half = KVH * HD
    for j in range(cycle_size):
        rows = partial[j * RCP : (j + 1) * RCP]
        red_send[j] = jnp.concatenate([rows[:, :half], rows[:, half:]], axis=0).astype(bf16)

    def r_copy(peer):
        return pltpu.make_async_remote_copy(
            src_ref=red_send.at[peer],
            dst_ref=red_recv.at[me],
            send_sem=r_sent.at[peer],
            recv_sem=r_came.at[me],
            device_id={"ctx": peer},
            device_id_type=MESH,
        )

    @pl.loop(1, cycle_size)
    def _(step):
        r_copy(lax.rem(me + step, cycle_size)).start()

    red_recv[me] = red_send[me]

    @pl.loop(1, KVH)
    def _(h):
        @pl.loop(0, me)
        def _(peer):
            q_copy(h, peer).start()

    for h in range(KVH):
        every_query[h, me] = queries[h]

    def store_own(h, k, part, block):
        slots[h, me_o * CAP + k, :, part * HD : (part + 1) * HD] = block

    pack(me_o, store_own)

    my_count = counts[me_o]
    query_total = cycle_size * RCP
    block_total = mask_cols.shape[0]
    index_of = lax.broadcasted_iota(jnp.int32, (query_total, 1), 0) // RCP
    own_place = position_col[...]
    query_pos = index_of * CTX_DEV + own_place
    query_block = index_of * NBD + own_place // BLK
    onehot = (
        lax.broadcasted_iota(jnp.int32, (query_total, block_total), 1) == query_block
    ).astype(f32).astype(bf16)
    lane = lax.broadcasted_iota(jnp.int32, (query_total, BLK), 1)
    mask_float = mask_cols[...].astype(f32)
    for b in range(NBD):
        column = jnp.broadcast_to(mask_float[:, b : b + 1], (block_total, BLK)).astype(bf16)
        allowed = jnp.dot(onehot, column, preferred_element_type=f32)
        key_block = me * NBD + b
        last = jnp.where(key_block < my_count, query_pos, -1)
        seen = (allowed > 0.5) & (key_block * BLK + lane <= last)
        bias[:, b * BLK : (b + 1) * BLK] = jnp.where(seen, 0.0, HIDDEN)

    values_ones[:, HD:] = jnp.ones((CTX_DEV, HD), bf16)

    @pl.loop(1, cycle_size)
    def _(step):
        source = lax.rem(me + step, cycle_size)
        pltpu.make_async_remote_copy(
            src_ref=red_send.at[source],
            dst_ref=red_recv.at[source],
            send_sem=r_sent.at[source],
            recv_sem=r_came.at[source],
            device_id={"ctx": source},
            device_id_type=MESH,
        ).wait_recv()

    total = red_recv[0].astype(f32)
    for c in range(1, cycle_size):
        total = total + red_recv[c].astype(f32)
    fresh[...] = jnp.zeros((KVH, BLK, 2 * HD), bf16)
    for h in range(KVH):
        columns = slice(h * HD, (h + 1) * HD)
        rows = jnp.concatenate([total[:RCP, columns], total[RCP:, columns]], axis=1)
        fresh[h, : 2 * RCP] = jnp.concatenate([rows, jnp.zeros_like(rows)], axis=0).astype(bf16)

    place_lane = lax.broadcasted_iota(jnp.int32, (1, BLK), 1)
    place_row = jnp.full((1, BLK), -1, jnp.int32)
    for i in range(RCP):
        place_row = jnp.where(place_lane == i, positions[0, me * RCP + i], place_row)

    where_from = []
    for b in range(NBD):
        source = lax.div(retrieval[me_o, b], group_size)
        ordinal = jnp.int32(0)
        for a in range(b):
            same = (lax.div(retrieval[me_o, a], group_size) == source) & (
                me * NBD + a < my_count
            )
            ordinal = ordinal + jnp.where(same, 1, 0)
        where_from.append(source * CAP + jnp.minimum(ordinal, CAP - 1))

    def combine(h):
        @pl.loop(0, me)
        def _(source):
            pltpu.make_async_remote_copy(
                src_ref=part_send.at[h, source],
                dst_ref=part_recv.at[h, source],
                send_sem=p_sent.at[h, source],
                recv_sem=p_came.at[h, source],
                device_id={"ctx": source},
                device_id_type=MESH,
            ).wait_recv()

        for c in range(cycle_size):
            pieces = part_recv[h, c, ROWS:, :].astype(f32)
            level = jnp.sum(pieces, axis=0, keepdims=True)
            levels[c : c + 1, :] = jnp.where(c <= me, level, 2 * HIDDEN)
        level = levels[...]
        share = jnp.exp2(level - jnp.max(level, axis=0, keepdims=True))
        share = share / jnp.sum(share, axis=0, keepdims=True)
        if cycle_size < BLK:
            share = jnp.concatenate(
                [share, jnp.zeros((BLK - cycle_size, BLK), f32)], axis=0
            )
        shares[...] = share.T
        mine = shares[pl.ds(lax.rem(me, 2) * ROWS, ROWS), :]
        result = jnp.zeros((ROWS, HD), f32)
        for c in range(cycle_size):
            part = jnp.where(c <= me, part_recv[h, c, :ROWS, :].astype(f32), 0.0)
            result = result + part * mine[:, c : c + 1]
        attended[h] = result.astype(bf16)

    @pl.loop(0, KVH)
    def _(h):
        @pl.loop(1, owner_count)
        def _(step):
            source = lax.rem(me_o + step, owner_count)
            pltpu.make_async_remote_copy(
                src_ref=x_send.at[h, source],
                dst_ref=slots.at[h, pl.ds(source * CAP, CAP)],
                send_sem=x_sent.at[h, source],
                recv_sem=x_came.at[h, source],
                device_id={"owner": source},
                device_id_type=MESH,
            ).wait_recv()

        key_columns = pl.ds(pl.multiple_of(h * HD, HD), HD)
        value_columns = pl.ds(pl.multiple_of((KVH + h) * HD, HD), HD)
        fresh_rows = fresh[h]
        stage[...] = slots[h]
        for b in range(NBD):
            rows = slice(b * BLK, (b + 1) * BLK)
            match = (
                lax.broadcasted_iota(jnp.int32, (BLK, BLK), 0) + b * BLK == place_row
            ).astype(f32)
            replaced = jnp.sum(match, axis=1, keepdims=True) > 0.5
            placed = jnp.dot(match.astype(bf16), fresh_rows, preferred_element_type=f32)
            block = stage[where_from[b]].astype(f32)
            block = jnp.where(me * NBD + b < my_count, block, 0.0)
            block = jnp.where(replaced, placed, block).astype(bf16)
            context[rows, key_columns] = block[:, :HD]
            context[rows, value_columns] = block[:, HD:]
            values_ones[rows, :HD] = block[:, HD:]

        @pl.loop(me + 1, cycle_size)
        def _(source):
            pltpu.make_async_remote_copy(
                src_ref=queries.at[h],
                dst_ref=every_query.at[h, source],
                send_sem=q_sent.at[h, source],
                recv_sem=q_came.at[h, source],
                device_id={"ctx": source},
                device_id_type=MESH,
            ).wait_recv()

        @pl.loop(lax.div(me, TILE), cycle_size // TILE)
        def _(tile):
            query_rows = every_query[h, pl.ds(tile * TILE, TILE)].reshape(TILE * ROWS, HD)
            scores = lax.dot_general(
                query_rows,
                context[:, key_columns],
                (((1,), (1,)), ((), ())),
                preferred_element_type=f32,
            )
            shift = bias[pl.ds(pl.multiple_of(tile * TILE * RCP, TILE * RCP), TILE * RCP), :]
            scores = scores.reshape(TILE, GROUP, RCP, CTX_DEV) + shift.reshape(
                TILE, 1, RCP, CTX_DEV
            )
            scores = scores.reshape(TILE * ROWS, CTX_DEV)
            highest = jnp.max(scores, axis=1, keepdims=True)
            weights = jnp.exp2((scores - highest) * FACTOR).astype(bf16)
            summed = jnp.dot(weights, values_ones[...], preferred_element_type=f32)
            weight_sum = summed[:, HD:]
            outcome = (summed[:, :HD] / weight_sum).astype(bf16)
            level = highest * FACTOR + jnp.log(weight_sum) * LOG2E
            level = level.T[:STAT]
            high = level.astype(bf16).astype(f32)
            middle = (level - high).astype(bf16).astype(f32)
            low = level - high - middle
            row = lax.broadcasted_iota(jnp.int32, level.shape, 0)
            stat = jnp.where(
                row == 0, high, jnp.where(row == 1, middle, jnp.where(row == 2, low, 0.0))
            ).astype(bf16)
            for jj in range(TILE):
                j = tile * TILE + jj
                pair = jj // 2
                part = outcome[jj * ROWS : (jj + 1) * ROWS]
                stat_part = stat[:, pair * BLK : (pair + 1) * BLK]

                @pl.when(j > me)
                def _():
                    part_send[h, j, :ROWS, :] = part
                    part_send[h, j, ROWS:, :] = stat_part
                    pltpu.make_async_remote_copy(
                        src_ref=part_send.at[h, j],
                        dst_ref=part_recv.at[h, me],
                        send_sem=p_sent.at[h, j],
                        recv_sem=p_came.at[h, me],
                        device_id={"ctx": j},
                        device_id_type=MESH,
                    ).start()

                @pl.when(j == me)
                def _():
                    part_recv[h, me, :ROWS, :] = part
                    part_recv[h, me, ROWS:, :] = stat_part

        @pl.when(h > 0)
        def _():
            combine(h - 1)

    combine(KVH - 1)

    @pl.loop(0, KVH)
    def _(h):
        @pl.loop(1, owner_count)
        def _(step):
            x_copy(h, step).wait_send()

        @pl.loop(0, me)
        def _(peer):
            q_copy(h, peer).wait_send()

        @pl.loop(me + 1, cycle_size)
        def _(j):
            pltpu.make_async_remote_copy(
                src_ref=part_send.at[h, j],
                dst_ref=part_recv.at[h, me],
                send_sem=p_sent.at[h, j],
                recv_sem=p_came.at[h, me],
                device_id={"ctx": j},
                device_id_type=MESH,
            ).wait_send()

    @pl.loop(1, cycle_size)
    def _(step):
        r_copy(lax.rem(me + step, cycle_size)).wait_send()


def on_device(span_cache, retrieval, counts, recompute_pos, hidden, kv_weight, queries, block_mask):
    owner_count = lax.axis_size("owner")
    cycle_size = lax.axis_size("ctx")
    width = span_cache.shape[2]
    bf16 = jnp.bfloat16
    grouped = queries[0].reshape(RCP, KVH, GROUP, HD).transpose(1, 2, 0, 3)
    grouped = grouped.reshape(KVH, ROWS, HD)
    vmem = pl.BlockSpec(memory_space=pltpu.VMEM)
    smem = pl.BlockSpec(memory_space=pltpu.SMEM)
    dma = pltpu.SemaphoreType.DMA
    context, attended = pl.pallas_call(
        functools.partial(kernel, owner_count, cycle_size),
        out_shape=(
            jax.ShapeDtypeStruct((CTX_DEV, width), bf16),
            jax.ShapeDtypeStruct((KVH, ROWS, HD), bf16),
        ),
        in_specs=[smem] * 3 + [vmem] * 6,
        out_specs=(vmem, vmem),
        scratch_shapes=[
            pltpu.VMEM((KVH, owner_count, CAP, BLK, 2 * HD), bf16),
            pltpu.VMEM((KVH, owner_count * CAP, BLK, 2 * HD), bf16),
            pltpu.VMEM((owner_count * CAP, BLK, 2 * HD), bf16),
            pltpu.VMEM((KVH, cycle_size, ROWS, HD), bf16),
            pltpu.VMEM((cycle_size, 2 * RCP, KVH * HD), bf16),
            pltpu.VMEM((cycle_size, 2 * RCP, KVH * HD), bf16),
            pltpu.VMEM((KVH, BLK, 2 * HD), bf16),
            pltpu.VMEM((cycle_size * RCP, CTX_DEV), jnp.float32),
            pltpu.VMEM((CTX_DEV, 2 * HD), bf16),
            pltpu.VMEM((KVH, cycle_size, ROWS + STAT, HD), bf16),
            pltpu.VMEM((KVH, cycle_size, ROWS + STAT, HD), bf16),
            pltpu.VMEM((cycle_size, BLK), jnp.float32),
            pltpu.VMEM((BLK, BLK), jnp.float32),
            dma((KVH, owner_count)),
            dma((KVH, owner_count)),
            dma((KVH, cycle_size)),
            dma((KVH, cycle_size)),
            dma((cycle_size,)),
            dma((cycle_size,)),
            dma((KVH, cycle_size)),
            dma((KVH, cycle_size)),
        ],
        compiler_params=pltpu.CompilerParams(
            collective_id=0, has_side_effects=True, vmem_limit_bytes=56 * 1024 * 1024
        ),
        name="span_attention",
    )(
        retrieval,
        counts,
        recompute_pos,
        recompute_pos.reshape(-1, 1),
        block_mask[0],
        hidden[0],
        kv_weight,
        grouped,
        span_cache,
    )
    attended = attended.reshape(KVH, GROUP, RCP, HD).transpose(2, 0, 1, 3)
    return (context[None], attended.reshape(1, RCP, QH * HD))


def solution(mesh):
    in_specs = (
        P(("owner", "ctx"), None, None),
        P(None, "ctx"),
        P(),
        P("owner", None),
        P("owner", None, "ctx"),
        P("ctx", None),
        P("owner", "ctx", None),
        P("owner", None, "ctx"),
    )
    out_specs = (P("owner", "ctx", None), P("owner", "ctx", None))
    return jax.shard_map(
        on_device, mesh=mesh, in_specs=in_specs, out_specs=out_specs, check_vma=False
    )
```

```python
import functools

import jax
import jax.numpy as jnp
from jax import lax
from jax.experimental import pallas as pl
from jax.experimental.pallas import tpu as pltpu
from jax.sharding import PartitionSpec as P

QH = 32
KVH = 4
HD = 128
BLK = 128
NBD = 8
RCP = 8
SLOTS = 8
CAP = 4
CTX_DEV = 1024
GROUP = QH // KVH
ROWS = GROUP * RCP
TILE = 4
STAT = 16
HIDDEN = -1e30
LOG2E = 1.4426950408889634
FACTOR = HD ** (-0.5) * LOG2E
MESH = pl.DeviceIdType.MESH


def kernel(
    owner_count,
    cycle_size,
    retrieval,
    counts,
    positions,
    position_row,
    mask_rows,
    hidden,
    weight,
    queries,
    spans,
    context_out,
    attended,
    x_send,
    x_recv,
    own,
    stage,
    context,
    every_query,
    red_send,
    red_recv,
    fresh,
    bias,
    sums,
    tops,
    totals,
    part_send,
    part_recv,
    levels,
    shares,
    x_sent,
    x_came,
    q_sent,
    q_came,
    r_sent,
    r_came,
    p_sent,
    p_came,
    out_done,
):
    me_o = lax.axis_index("owner")
    me = lax.axis_index("ctx")
    group_size = cycle_size * SLOTS
    f32, bf16 = jnp.float32, jnp.bfloat16
    own_keys = CAP * BLK + BLK

    barrier = pltpu.get_barrier_semaphore()

    @pl.loop(1, cycle_size)
    def _(step):
        peer = lax.rem(me + step, cycle_size)
        pl.semaphore_signal(barrier, inc=1, device_id={"ctx": peer}, device_id_type=MESH)

    @pl.loop(1, owner_count)
    def _(step):
        peer = lax.rem(me_o + step, owner_count)
        pl.semaphore_signal(barrier, inc=1, device_id={"owner": peer}, device_id_type=MESH)

    def chosen_slots(request):
        count = counts[request]
        rank = jnp.int32(0)
        chosen = [jnp.int32(0)] * CAP
        for b in range(NBD):
            span = retrieval[request, b]
            mine = (me * NBD + b < count) & (lax.div(span, group_size) == me_o)
            for k in range(CAP):
                chosen[k] = jnp.where(mine & (rank == k), lax.rem(span, SLOTS), chosen[k])
            rank = rank + jnp.where(mine, 1, 0)
        return chosen

    def pack(chosen, heads, store):
        for h in heads:
            for k in range(CAP):
                for part in range(2):
                    column = (part * KVH + h) * HD
                    store(h, k, part, spans[chosen[k], :, column : column + HD])

    def x_copy(h, step):
        peer = lax.rem(me_o + step, owner_count)
        return pltpu.make_async_remote_copy(
            src_ref=x_send.at[h, peer],
            dst_ref=x_recv.at[h, me_o],
            send_sem=x_sent.at[h, peer],
            recv_sem=x_came.at[h, me_o],
            device_id={"owner": peer},
            device_id_type=MESH,
        )

    def x_start(h):
        @pl.loop(1, owner_count)
        def _(step):
            x_copy(h, step).start()

    def x_wait_send(h):
        @pl.loop(1, owner_count)
        def _(step):
            x_copy(h, step).wait_send()

    def pack_for_peers(heads):
        @pl.loop(1, owner_count)
        def _(step):
            peer = lax.rem(me_o + step, owner_count)

            def store(h, k, part, block):
                x_send[h, peer, k, :, part * HD : (part + 1) * HD] = block

            pack(chosen_slots(peer), heads, store)

    def q_copy(h, peer):
        return pltpu.make_async_remote_copy(
            src_ref=queries.at[h],
            dst_ref=every_query.at[h, me],
            send_sem=q_sent.at[h, peer],
            recv_sem=q_came.at[h, me],
            device_id={"ctx": peer},
            device_id_type=MESH,
        )

    def q_start(h):
        @pl.loop(0, me)
        def _(peer):
            q_copy(h, peer).start()

    def r_copy(peer):
        return pltpu.make_async_remote_copy(
            src_ref=red_send.at[peer],
            dst_ref=red_recv.at[me],
            send_sem=r_sent.at[peer],
            recv_sem=r_came.at[me],
            device_id={"ctx": peer},
            device_id_type=MESH,
        )

    pack_for_peers(range(1))
    pl.semaphore_wait(barrier, cycle_size + owner_count - 2)
    x_start(0)
    q_start(0)
    pack_for_peers(range(1, 2))
    x_start(1)

    partial = jnp.dot(hidden[...], weight[...], preferred_element_type=f32)
    half = KVH * HD
    for j in range(cycle_size):
        rows = partial[j * RCP : (j + 1) * RCP]
        red_send[j] = jnp.concatenate([rows[:, :half], rows[:, half:]], axis=0).astype(bf16)

    @pl.loop(1, cycle_size)
    def _(step):
        r_copy(lax.rem(me + step, cycle_size)).start()

    q_start(1)
    pack_for_peers(range(2, KVH))
    red_recv[me] = red_send[me]

    for h in range(KVH):
        every_query[h, me] = queries[h]

    def store_own(h, k, part, block):
        own[h, k * BLK : (k + 1) * BLK, part * HD : (part + 1) * HD] = block

    pack(chosen_slots(me_o), range(KVH), store_own)

    my_count = counts[me_o]
    query_total = cycle_size * RCP
    block_total = mask_rows.shape[1]

    where_from = []
    usable = []
    for b in range(NBD):
        source = lax.div(retrieval[me_o, b], group_size)
        ordinal = jnp.int32(0)
        for a in range(b):
            same = (lax.div(retrieval[me_o, a], group_size) == source) & (
                me * NBD + a < my_count
            )
            ordinal = ordinal + jnp.where(same, 1, 0)
        where_from.append(source * CAP + jnp.minimum(ordinal, CAP - 1))
        usable.append(me * NBD + b < my_count)

    place_lane = lax.broadcasted_iota(jnp.int32, (1, BLK), 1)
    place_row = jnp.full((1, BLK), -1, jnp.int32)
    for i in range(RCP):
        place_row = jnp.where(place_lane == i, positions[0, me * RCP + i], place_row)
    place_col = jnp.broadcast_to(place_row, (BLK, BLK)).astype(f32).T.astype(jnp.int32)[:, :1]
    block_lane = lax.broadcasted_iota(jnp.int32, (1, BLK), 1)

    index_of = lax.broadcasted_iota(jnp.int32, (1, query_total), 1) // RCP
    own_place = position_row[...]
    query_pos = index_of * CTX_DEV + own_place
    query_block = index_of * NBD + own_place // BLK
    onehot = (
        lax.broadcasted_iota(jnp.int32, (block_total, query_total), 0) == query_block
    ).astype(f32).astype(bf16)
    allowed = jnp.dot(
        mask_rows[...].astype(f32).astype(bf16), onehot, preferred_element_type=f32
    )
    block_row = lax.broadcasted_iota(jnp.int32, (NBD, query_total), 0) + me * NBD
    reach = jnp.where(
        (allowed > 0.5) & (block_row < my_count),
        (query_pos - block_row * BLK).astype(f32),
        -1.0,
    )

    def reach_columns(pieces):
        filled = jnp.concatenate(
            [jnp.broadcast_to(piece, (8, query_total)) for piece in pieces], axis=0
        )
        rest = query_total - filled.shape[0]
        if rest > 0:
            filled = jnp.concatenate([filled, jnp.zeros((rest, query_total), f32)], axis=0)
        return filled.T

    def slot_bias(owner):
        reached = []
        gone = []
        for k in range(CAP):
            slot = jnp.full((1, query_total), -1.0, f32)
            offset = jnp.int32(-1)
            for b in range(NBD):
                here = usable[b] & (where_from[b] == owner * CAP + k)
                slot = jnp.where(here, reach[b : b + 1], slot)
                offset = jnp.where(here, b * BLK, offset)
            reached.append(slot)
            match = (place_col + jnp.zeros((BLK, BLK), jnp.int32)) == block_lane + offset
            row = lax.broadcasted_iota(jnp.int32, (BLK, BLK), 0)
            hit = jnp.where(match & (row < RCP) & (offset >= 0), 1.0, 0.0)
            gone.append(jnp.max(hit, axis=0, keepdims=True))
        columns = reach_columns(reached)
        lanes = block_lane.astype(f32)
        for k in range(CAP):
            seen = (lanes <= columns[:, k * 8 : k * 8 + 1]) & (gone[k] < 0.5)
            bias[owner, :, k * BLK : (k + 1) * BLK] = jnp.where(seen, 0.0, HIDDEN)

    for o in range(owner_count):
        slot_bias(o)

    reached = []
    for i in range(RCP):
        place = positions[0, me * RCP + i]
        row = jnp.full((1, query_total), -1.0, f32)
        for b in range(NBD):
            here = lax.div(place, BLK) == b
            row = jnp.where(here, reach[b : b + 1] - (place - b * BLK).astype(f32), row)
        reached.append(row)
    columns = reach_columns(reached)
    shift = jnp.full((query_total, BLK), HIDDEN, f32)
    for i in range(RCP):
        seen = (columns[:, i * 8 : i * 8 + 1] >= 0.0) & (block_lane == i)
        shift = jnp.where(seen, 0.0, shift)
    bias[me_o, :, CAP * BLK :] = shift

    @pl.loop(1, cycle_size)
    def _(step):
        source = lax.rem(me + step, cycle_size)
        pltpu.make_async_remote_copy(
            src_ref=red_send.at[source],
            dst_ref=red_recv.at[source],
            send_sem=r_sent.at[source],
            recv_sem=r_came.at[source],
            device_id={"ctx": source},
            device_id_type=MESH,
        ).wait_recv()

    total = red_recv[0].astype(f32)
    for c in range(1, cycle_size):
        total = total + red_recv[c].astype(f32)
    fresh[...] = jnp.zeros((KVH, BLK, 2 * HD), bf16)
    for h in range(KVH):
        columns = slice(h * HD, (h + 1) * HD)
        rows = jnp.concatenate([total[:RCP, columns], total[RCP:, columns]], axis=1)
        fresh[h, : 2 * RCP] = jnp.concatenate([rows, jnp.zeros_like(rows)], axis=0).astype(bf16)
        own[h, CAP * BLK :] = fresh[h]

    q_start(2)

    def score(h, tile, keys, owner, key_count):
        query_rows = every_query[h, pl.ds(tile * TILE, TILE)].reshape(TILE * ROWS, HD)
        scores = lax.dot_general(
            query_rows, keys, (((1,), (1,)), ((), ())), preferred_element_type=f32
        )
        first = pl.multiple_of(tile * TILE * RCP, TILE * RCP)
        shift = bias[owner, pl.ds(first, TILE * RCP), :key_count]
        scores = scores.reshape(TILE, GROUP, RCP, key_count) + shift.reshape(
            TILE, 1, RCP, key_count
        )
        return scores.reshape(TILE * ROWS, key_count)

    def tile_rows(tile):
        return pl.ds(pl.multiple_of(tile * TILE * ROWS, TILE * ROWS), TILE * ROWS)

    def attend_own(h):
        @pl.loop(me + 1, cycle_size)
        def _(source):
            pltpu.make_async_remote_copy(
                src_ref=queries.at[h],
                dst_ref=every_query.at[h, source],
                send_sem=q_sent.at[h, source],
                recv_sem=q_came.at[h, source],
                device_id={"ctx": source},
                device_id_type=MESH,
            ).wait_recv()

        @pl.loop(lax.div(me, TILE), cycle_size // TILE)
        def _(tile):
            scores = score(h, tile, own[h, :, :HD], me_o, own_keys)
            highest = jnp.max(scores, axis=1, keepdims=True)
            weights = jnp.exp2((scores - highest) * FACTOR)
            rows = tile_rows(tile)
            totals[h, rows] = jnp.broadcast_to(
                jnp.sum(weights, axis=1, keepdims=True), (TILE * ROWS, HD)
            )
            tops[h, rows] = jnp.broadcast_to(highest, (TILE * ROWS, HD))
            sums[h, rows] = jnp.dot(
                weights.astype(bf16), own[h, :, HD:], preferred_element_type=f32
            )

    def attend_others(h):
        @pl.loop(1, owner_count)
        def _(step):
            source = lax.rem(me_o + step, owner_count)
            pltpu.make_async_remote_copy(
                src_ref=x_send.at[h, source],
                dst_ref=x_recv.at[h, source],
                send_sem=x_sent.at[h, source],
                recv_sem=x_came.at[h, source],
                device_id={"owner": source},
                device_id_type=MESH,
            ).wait_recv()

        @pl.loop(lax.div(me, TILE), cycle_size // TILE)
        def _(tile):
            rows = tile_rows(tile)
            highest, weight_sum, summed = tops[h, rows], totals[h, rows], sums[h, rows]
            for step in range(1, owner_count):
                source = lax.rem(me_o + step, owner_count)
                block = x_recv.at[h, source]
                keys = block[:, :, :HD].reshape(CAP * BLK, HD)
                scores = score(h, tile, keys, source, CAP * BLK)
                newest = jnp.maximum(highest[:, :1], jnp.max(scores, axis=1, keepdims=True))
                weights = jnp.exp2((scores - newest) * FACTOR)
                factor = jnp.exp2((highest - newest) * FACTOR)
                weight_sum = weight_sum * factor + jnp.sum(weights, axis=1, keepdims=True)
                values = block[:, :, HD:].reshape(CAP * BLK, HD)
                summed = summed * factor + jnp.dot(
                    weights.astype(bf16), values, preferred_element_type=f32
                )
                highest = jnp.broadcast_to(newest, (TILE * ROWS, HD))
            outcome = (summed / weight_sum).astype(bf16)
            level = highest * FACTOR + jnp.log(weight_sum) * LOG2E
            level = level.T[:STAT]
            high = level.astype(bf16).astype(f32)
            middle = (level - high).astype(bf16).astype(f32)
            low = level - high - middle
            row = lax.broadcasted_iota(jnp.int32, level.shape, 0)
            stat = jnp.where(
                row == 0, high, jnp.where(row == 1, middle, jnp.where(row == 2, low, 0.0))
            ).astype(bf16)
            for jj in range(TILE):
                j = tile * TILE + jj
                pair = jj // 2
                part = outcome[jj * ROWS : (jj + 1) * ROWS]
                stat_part = stat[:, pair * BLK : (pair + 1) * BLK]

                @pl.when(j > me)
                def _():
                    part_send[h, j, :ROWS, :] = part
                    part_send[h, j, ROWS:, :] = stat_part
                    p_copy(h, j).start()

                @pl.when(j == me)
                def _():
                    part_recv[h, me, :ROWS, :] = part
                    part_recv[h, me, ROWS:, :] = stat_part

    def p_copy(h, j):
        return pltpu.make_async_remote_copy(
            src_ref=part_send.at[h, j],
            dst_ref=part_recv.at[h, me],
            send_sem=p_sent.at[h, j],
            recv_sem=p_came.at[h, me],
            device_id={"ctx": j},
            device_id_type=MESH,
        )

    def out_copies(h):
        for part in range(2):
            columns = pl.ds(pl.multiple_of((part * KVH + h) * HD, HD), HD)
            yield pltpu.make_async_copy(
                context.at[:, columns], context_out.at[:, columns], out_done.at[h, part]
            )

    def assemble(h):
        @pl.loop(1, owner_count)
        def _(step):
            source = lax.rem(me_o + step, owner_count)
            stage[pl.ds(source * CAP, CAP)] = x_recv[h, source]

        stage[pl.ds(me_o * CAP, CAP)] = own[h, : CAP * BLK].reshape(CAP, BLK, 2 * HD)
        fresh_rows = fresh[h]
        for b in range(NBD):
            rows = slice(b * BLK, (b + 1) * BLK)
            match = (
                lax.broadcasted_iota(jnp.int32, (BLK, BLK), 0) + b * BLK == place_row
            ).astype(f32)
            replaced = jnp.sum(match, axis=1, keepdims=True) > 0.5
            placed = jnp.dot(match.astype(bf16), fresh_rows, preferred_element_type=f32)
            block = stage[where_from[b]].astype(f32)
            block = jnp.where(usable[b], block, 0.0)
            block = jnp.where(replaced, placed, block).astype(bf16)
            context[rows, pl.ds(pl.multiple_of(h * HD, HD), HD)] = block[:, :HD]
            context[rows, pl.ds(pl.multiple_of((KVH + h) * HD, HD), HD)] = block[:, HD:]
        for copy in out_copies(h):
            copy.start()

    def combine(h):
        @pl.loop(0, me)
        def _(source):
            pltpu.make_async_remote_copy(
                src_ref=part_send.at[h, source],
                dst_ref=part_recv.at[h, source],
                send_sem=p_sent.at[h, source],
                recv_sem=p_came.at[h, source],
                device_id={"ctx": source},
                device_id_type=MESH,
            ).wait_recv()

        for c in range(cycle_size):
            pieces = part_recv[h, c, ROWS:, :].astype(f32)
            level = jnp.sum(pieces, axis=0, keepdims=True)
            levels[c : c + 1, :] = jnp.where(c <= me, level, 2 * HIDDEN)
        level = levels[...]
        share = jnp.exp2(level - jnp.max(level, axis=0, keepdims=True))
        share = share / jnp.sum(share, axis=0, keepdims=True)
        if cycle_size < BLK:
            share = jnp.concatenate(
                [share, jnp.zeros((BLK - cycle_size, BLK), f32)], axis=0
            )
        shares[...] = share.T
        mine = shares[pl.ds(lax.rem(me, 2) * ROWS, ROWS), :]
        result = jnp.zeros((ROWS, HD), f32)
        for c in range(cycle_size):
            part = jnp.where(c <= me, part_recv[h, c, :ROWS, :].astype(f32), 0.0)
            result = result + part * mine[:, c : c + 1]
        attended[h] = result.astype(bf16)

    attend_own(0)
    q_start(3)
    attend_own(1)
    x_wait_send(0)
    x_start(2)
    attend_others(0)
    x_wait_send(1)
    x_start(3)

    @pl.loop(1, KVH)
    def _(h):
        @pl.when(h < KVH - 1)
        def _():
            attend_own(h + 1)

        assemble(h - 1)
        attend_others(h)
        combine(h - 1)

    assemble(KVH - 1)
    combine(KVH - 1)

    x_wait_send(2)
    x_wait_send(3)

    @pl.loop(0, KVH)
    def _(h):
        for copy in out_copies(h):
            copy.wait()

        @pl.loop(0, me)
        def _(peer):
            q_copy(h, peer).wait_send()

        @pl.loop(me + 1, cycle_size)
        def _(j):
            p_copy(h, j).wait_send()

    @pl.loop(1, cycle_size)
    def _(step):
        r_copy(lax.rem(me + step, cycle_size)).wait_send()


def on_device(span_cache, retrieval, counts, recompute_pos, hidden, kv_weight, queries, block_mask):
    owner_count = lax.axis_size("owner")
    cycle_size = lax.axis_size("ctx")
    width = span_cache.shape[2]
    bf16, f32 = jnp.bfloat16, jnp.float32
    grouped = queries[0].reshape(RCP, KVH, GROUP, HD).transpose(1, 2, 0, 3)
    grouped = grouped.reshape(KVH, ROWS, HD)
    vmem = pl.BlockSpec(memory_space=pltpu.VMEM)
    smem = pl.BlockSpec(memory_space=pltpu.SMEM)
    dma = pltpu.SemaphoreType.DMA
    context, attended = pl.pallas_call(
        functools.partial(kernel, owner_count, cycle_size),
        out_shape=(
            jax.ShapeDtypeStruct((CTX_DEV, width), bf16),
            jax.ShapeDtypeStruct((KVH, ROWS, HD), bf16),
        ),
        in_specs=[smem] * 3 + [vmem] * 6,
        out_specs=(pl.BlockSpec(memory_space=pl.ANY), vmem),
        scratch_shapes=[
            pltpu.VMEM((KVH, owner_count, CAP, BLK, 2 * HD), bf16),
            pltpu.VMEM((KVH, owner_count, CAP, BLK, 2 * HD), bf16),
            pltpu.VMEM((KVH, CAP * BLK + BLK, 2 * HD), bf16),
            pltpu.VMEM((owner_count * CAP, BLK, 2 * HD), bf16),
            pltpu.VMEM((CTX_DEV, width), bf16),
            pltpu.VMEM((KVH, cycle_size, ROWS, HD), bf16),
            pltpu.VMEM((cycle_size, 2 * RCP, KVH * HD), bf16),
            pltpu.VMEM((cycle_size, 2 * RCP, KVH * HD), bf16),
            pltpu.VMEM((KVH, BLK, 2 * HD), bf16),
            pltpu.VMEM((owner_count, cycle_size * RCP, CAP * BLK + BLK), f32),
            pltpu.VMEM((KVH, cycle_size * ROWS, HD), f32),
            pltpu.VMEM((KVH, cycle_size * ROWS, HD), f32),
            pltpu.VMEM((KVH, cycle_size * ROWS, HD), f32),
            pltpu.VMEM((KVH, cycle_size, ROWS + STAT, HD), bf16),
            pltpu.VMEM((KVH, cycle_size, ROWS + STAT, HD), bf16),
            pltpu.VMEM((cycle_size, BLK), f32),
            pltpu.VMEM((BLK, BLK), f32),
            dma((KVH, owner_count)),
            dma((KVH, owner_count)),
            dma((KVH, cycle_size)),
            dma((KVH, cycle_size)),
            dma((cycle_size,)),
            dma((cycle_size,)),
            dma((KVH, cycle_size)),
            dma((KVH, cycle_size)),
            dma((KVH, 2)),
        ],
        compiler_params=pltpu.CompilerParams(
            collective_id=0, has_side_effects=True, vmem_limit_bytes=56 * 1024 * 1024
        ),
        name="span_attention",
    )(
        retrieval,
        counts,
        recompute_pos,
        recompute_pos,
        block_mask[0].T,
        hidden[0],
        kv_weight,
        grouped,
        span_cache,
    )
    attended = attended.reshape(KVH, GROUP, RCP, HD).transpose(2, 0, 1, 3)
    return (context[None], attended.reshape(1, RCP, QH * HD))


def solution(mesh):
    in_specs = (
        P(("owner", "ctx"), None, None),
        P(None, "ctx"),
        P(),
        P("owner", None),
        P("owner", None, "ctx"),
        P("ctx", None),
        P("owner", "ctx", None),
        P("owner", None, "ctx"),
    )
    out_specs = (P("owner", "ctx", None), P("owner", "ctx", None))
    return jax.shard_map(
        on_device, mesh=mesh, in_specs=in_specs, out_specs=out_specs, check_vma=False
    )
```

```python
import functools

import jax
import jax.numpy as jnp
from jax import lax
from jax.experimental import pallas as pl
from jax.experimental.pallas import tpu as pltpu
from jax.sharding import PartitionSpec as P

QH = 32
KVH = 4
HD = 128
BLK = 128
NBD = 8
RCP = 8
SLOTS = 8
CAP = 4
CTX_DEV = 1024
GROUP = QH // KVH
ROWS = GROUP * RCP
TILE = 4
STAT = 16
HIDDEN = -1e30
LOG2E = 1.4426950408889634
FACTOR = HD ** (-0.5) * LOG2E
MESH = pl.DeviceIdType.MESH


def kernel(
    owner_count,
    cycle_size,
    retrieval,
    counts,
    positions,
    position_row,
    mask_rows,
    hidden,
    weight,
    queries,
    spans,
    context_out,
    attended,
    x_send,
    x_recv,
    own,
    own_turned,
    others_turned,
    stage,
    context,
    every_query,
    red_send,
    red_recv,
    fresh,
    bias,
    sums,
    tops,
    totals,
    part_send,
    part_recv,
    levels,
    shares,
    x_sent,
    x_came,
    q_sent,
    q_came,
    r_sent,
    r_came,
    p_sent,
    p_came,
    out_done,
):
    me_o = lax.axis_index("owner")
    me = lax.axis_index("ctx")
    group_size = cycle_size * SLOTS
    f32, bf16 = jnp.float32, jnp.bfloat16
    own_keys = CAP * BLK + BLK

    barrier = pltpu.get_barrier_semaphore()

    @pl.loop(1, cycle_size)
    def _(step):
        peer = lax.rem(me + step, cycle_size)
        pl.semaphore_signal(barrier, inc=1, device_id={"ctx": peer}, device_id_type=MESH)

    @pl.loop(1, owner_count)
    def _(step):
        peer = lax.rem(me_o + step, owner_count)
        pl.semaphore_signal(barrier, inc=1, device_id={"owner": peer}, device_id_type=MESH)

    def chosen_slots(request):
        count = counts[request]
        rank = jnp.int32(0)
        chosen = [jnp.int32(0)] * CAP
        for b in range(NBD):
            span = retrieval[request, b]
            mine = (me * NBD + b < count) & (lax.div(span, group_size) == me_o)
            for k in range(CAP):
                chosen[k] = jnp.where(mine & (rank == k), lax.rem(span, SLOTS), chosen[k])
            rank = rank + jnp.where(mine, 1, 0)
        return chosen

    def pack(chosen, heads, store):
        for h in heads:
            for k in range(CAP):
                for part in range(2):
                    column = (part * KVH + h) * HD
                    store(h, k, part, spans[chosen[k], :, column : column + HD])

    def x_copy(h, step):
        peer = lax.rem(me_o + step, owner_count)
        return pltpu.make_async_remote_copy(
            src_ref=x_send.at[h, peer],
            dst_ref=x_recv.at[h, me_o],
            send_sem=x_sent.at[h, peer],
            recv_sem=x_came.at[h, me_o],
            device_id={"owner": peer},
            device_id_type=MESH,
        )

    def x_start(h):
        @pl.loop(1, owner_count)
        def _(step):
            x_copy(h, step).start()

    def x_wait_send(h):
        @pl.loop(1, owner_count)
        def _(step):
            x_copy(h, step).wait_send()

    def pack_for_peers(heads):
        @pl.loop(1, owner_count)
        def _(step):
            peer = lax.rem(me_o + step, owner_count)

            def store(h, k, part, block):
                x_send[h, peer, k, :, part * HD : (part + 1) * HD] = block

            pack(chosen_slots(peer), heads, store)

    def q_copy(h, peer):
        return pltpu.make_async_remote_copy(
            src_ref=queries.at[h],
            dst_ref=every_query.at[h, me],
            send_sem=q_sent.at[h, peer],
            recv_sem=q_came.at[h, me],
            device_id={"ctx": peer},
            device_id_type=MESH,
        )

    def q_start(h):
        @pl.loop(0, me)
        def _(peer):
            q_copy(h, peer).start()

    def r_copy(peer):
        return pltpu.make_async_remote_copy(
            src_ref=red_send.at[peer],
            dst_ref=red_recv.at[me],
            send_sem=r_sent.at[peer],
            recv_sem=r_came.at[me],
            device_id={"ctx": peer},
            device_id_type=MESH,
        )

    pack_for_peers(range(1))
    pl.semaphore_wait(barrier, cycle_size + owner_count - 2)
    x_start(0)
    q_start(0)
    pack_for_peers(range(1, KVH))
    for h in range(1, KVH):
        x_start(h)

    partial = jnp.dot(hidden[...], weight[...], preferred_element_type=f32)
    half = KVH * HD
    for j in range(cycle_size):
        rows = partial[j * RCP : (j + 1) * RCP]
        red_send[j] = jnp.concatenate([rows[:, :half], rows[:, half:]], axis=0).astype(bf16)

    @pl.loop(1, cycle_size)
    def _(step):
        r_copy(lax.rem(me + step, cycle_size)).start()

    for h in range(1, KVH):
        q_start(h)

    red_recv[me] = red_send[me]

    for h in range(KVH):
        every_query[h, me] = queries[h]

    def store_own(h, k, part, block):
        own[h, k * BLK : (k + 1) * BLK, part * HD : (part + 1) * HD] = block

    pack(chosen_slots(me_o), range(KVH), store_own)

    my_count = counts[me_o]
    query_total = cycle_size * RCP
    block_total = mask_rows.shape[1]

    where_from = []
    usable = []
    for b in range(NBD):
        source = lax.div(retrieval[me_o, b], group_size)
        ordinal = jnp.int32(0)
        for a in range(b):
            same = (lax.div(retrieval[me_o, a], group_size) == source) & (
                me * NBD + a < my_count
            )
            ordinal = ordinal + jnp.where(same, 1, 0)
        where_from.append(source * CAP + jnp.minimum(ordinal, CAP - 1))
        usable.append(me * NBD + b < my_count)

    place_lane = lax.broadcasted_iota(jnp.int32, (1, BLK), 1)
    place_row = jnp.full((1, BLK), -1, jnp.int32)
    for i in range(RCP):
        place_row = jnp.where(place_lane == i, positions[0, me * RCP + i], place_row)
    place_col = jnp.broadcast_to(place_row, (BLK, BLK)).astype(f32).T.astype(jnp.int32)[:, :1]
    block_lane = lax.broadcasted_iota(jnp.int32, (1, BLK), 1)

    index_of = lax.broadcasted_iota(jnp.int32, (1, query_total), 1) // RCP
    own_place = position_row[...]
    query_pos = index_of * CTX_DEV + own_place
    query_block = index_of * NBD + own_place // BLK
    onehot = (
        lax.broadcasted_iota(jnp.int32, (block_total, query_total), 0) == query_block
    ).astype(f32).astype(bf16)
    allowed = jnp.dot(
        mask_rows[...].astype(f32).astype(bf16), onehot, preferred_element_type=f32
    )
    block_row = lax.broadcasted_iota(jnp.int32, (NBD, query_total), 0) + me * NBD
    reach = jnp.where(
        (allowed > 0.5) & (block_row < my_count),
        (query_pos - block_row * BLK).astype(f32),
        -1.0,
    )

    def reach_columns(pieces):
        filled = jnp.concatenate(
            [jnp.broadcast_to(piece, (8, query_total)) for piece in pieces], axis=0
        )
        rest = query_total - filled.shape[0]
        if rest > 0:
            filled = jnp.concatenate([filled, jnp.zeros((rest, query_total), f32)], axis=0)
        return filled.T

    def slot_bias(owner):
        reached = []
        gone = []
        for k in range(CAP):
            slot = jnp.full((1, query_total), -1.0, f32)
            offset = jnp.int32(-1)
            for b in range(NBD):
                here = usable[b] & (where_from[b] == owner * CAP + k)
                slot = jnp.where(here, reach[b : b + 1], slot)
                offset = jnp.where(here, b * BLK, offset)
            reached.append(slot)
            match = (place_col + jnp.zeros((BLK, BLK), jnp.int32)) == block_lane + offset
            row = lax.broadcasted_iota(jnp.int32, (BLK, BLK), 0)
            hit = jnp.where(match & (row < RCP) & (offset >= 0), 1.0, 0.0)
            gone.append(jnp.max(hit, axis=0, keepdims=True))
        columns = reach_columns(reached)
        lanes = block_lane.astype(f32)
        for k in range(CAP):
            seen = (lanes <= columns[:, k * 8 : k * 8 + 1]) & (gone[k] < 0.5)
            bias[owner, :, k * BLK : (k + 1) * BLK] = jnp.where(seen, 0.0, HIDDEN)

    for o in range(owner_count):
        slot_bias(o)

    reached = []
    for i in range(RCP):
        place = positions[0, me * RCP + i]
        row = jnp.full((1, query_total), -1.0, f32)
        for b in range(NBD):
            here = lax.div(place, BLK) == b
            row = jnp.where(here, reach[b : b + 1] - (place - b * BLK).astype(f32), row)
        reached.append(row)
    columns = reach_columns(reached)
    shift = jnp.full((query_total, BLK), HIDDEN, f32)
    for i in range(RCP):
        seen = (columns[:, i * 8 : i * 8 + 1] >= 0.0) & (block_lane == i)
        shift = jnp.where(seen, 0.0, shift)
    bias[me_o, :, CAP * BLK :] = shift

    @pl.loop(1, cycle_size)
    def _(step):
        source = lax.rem(me + step, cycle_size)
        pltpu.make_async_remote_copy(
            src_ref=red_send.at[source],
            dst_ref=red_recv.at[source],
            send_sem=r_sent.at[source],
            recv_sem=r_came.at[source],
            device_id={"ctx": source},
            device_id_type=MESH,
        ).wait_recv()

    total = red_recv[0].astype(f32)
    for c in range(1, cycle_size):
        total = total + red_recv[c].astype(f32)
    fresh[...] = jnp.zeros((KVH, BLK, 2 * HD), bf16)
    for h in range(KVH):
        columns = slice(h * HD, (h + 1) * HD)
        rows = jnp.concatenate([total[:RCP, columns], total[RCP:, columns]], axis=1)
        fresh[h, : 2 * RCP] = jnp.concatenate([rows, jnp.zeros_like(rows)], axis=0).astype(bf16)
        own[h, CAP * BLK :] = fresh[h]

    def score(h, tile, keys, owner, key_count):
        query_rows = every_query[h, pl.ds(tile * TILE, TILE)].reshape(TILE * ROWS, HD)
        scores = lax.dot_general(
            query_rows, keys, (((1,), (0,)), ((), ())), preferred_element_type=f32
        )
        first = pl.multiple_of(tile * TILE * RCP, TILE * RCP)
        shift = bias[owner, pl.ds(first, TILE * RCP), :key_count]
        scores = scores.reshape(TILE, GROUP, RCP, key_count) + shift.reshape(
            TILE, 1, RCP, key_count
        )
        return scores.reshape(TILE * ROWS, key_count)

    def tile_rows(tile):
        return pl.ds(pl.multiple_of(tile * TILE * ROWS, TILE * ROWS), TILE * ROWS)

    def attend_own(h):
        @pl.loop(me + 1, cycle_size)
        def _(source):
            pltpu.make_async_remote_copy(
                src_ref=queries.at[h],
                dst_ref=every_query.at[h, source],
                send_sem=q_sent.at[h, source],
                recv_sem=q_came.at[h, source],
                device_id={"ctx": source},
                device_id_type=MESH,
            ).wait_recv()

        own_turned[...] = own[h, :, :HD].astype(f32).T.astype(bf16)

        @pl.loop(lax.div(me, TILE), cycle_size // TILE)
        def _(tile):
            scores = score(h, tile, own_turned[...], me_o, own_keys)
            highest = jnp.max(scores, axis=1, keepdims=True)
            weights = jnp.exp2((scores - highest) * FACTOR)
            rows = tile_rows(tile)
            totals[h, rows] = jnp.broadcast_to(
                jnp.sum(weights, axis=1, keepdims=True), (TILE * ROWS, HD)
            )
            tops[h, rows] = jnp.broadcast_to(highest, (TILE * ROWS, HD))
            sums[h, rows] = jnp.dot(
                weights.astype(bf16), own[h, :, HD:], preferred_element_type=f32
            )

    def attend_others(h):
        @pl.loop(1, owner_count)
        def _(step):
            source = lax.rem(me_o + step, owner_count)
            pltpu.make_async_remote_copy(
                src_ref=x_send.at[h, source],
                dst_ref=x_recv.at[h, source],
                send_sem=x_sent.at[h, source],
                recv_sem=x_came.at[h, source],
                device_id={"owner": source},
                device_id_type=MESH,
            ).wait_recv()
            keys = x_recv[h, source, :, :, :HD].reshape(CAP * BLK, HD)
            others_turned[source] = keys.astype(f32).T.astype(bf16)

        @pl.loop(lax.div(me, TILE), cycle_size // TILE)
        def _(tile):
            rows = tile_rows(tile)
            highest, weight_sum, summed = tops[h, rows], totals[h, rows], sums[h, rows]
            for step in range(1, owner_count):
                source = lax.rem(me_o + step, owner_count)
                block = x_recv.at[h, source]
                scores = score(h, tile, others_turned[source], source, CAP * BLK)
                newest = jnp.maximum(highest[:, :1], jnp.max(scores, axis=1, keepdims=True))
                weights = jnp.exp2((scores - newest) * FACTOR)
                factor = jnp.exp2((highest - newest) * FACTOR)
                weight_sum = weight_sum * factor + jnp.sum(weights, axis=1, keepdims=True)
                values = block[:, :, HD:].reshape(CAP * BLK, HD)
                summed = summed * factor + jnp.dot(
                    weights.astype(bf16), values, preferred_element_type=f32
                )
                highest = jnp.broadcast_to(newest, (TILE * ROWS, HD))
            outcome = (summed / weight_sum).astype(bf16)
            level = highest * FACTOR + jnp.log(weight_sum) * LOG2E
            level = level.T[:STAT]
            high = level.astype(bf16).astype(f32)
            middle = (level - high).astype(bf16).astype(f32)
            low = level - high - middle
            row = lax.broadcasted_iota(jnp.int32, level.shape, 0)
            stat = jnp.where(
                row == 0, high, jnp.where(row == 1, middle, jnp.where(row == 2, low, 0.0))
            ).astype(bf16)
            for jj in range(TILE):
                j = tile * TILE + jj
                pair = jj // 2
                part = outcome[jj * ROWS : (jj + 1) * ROWS]
                stat_part = stat[:, pair * BLK : (pair + 1) * BLK]

                @pl.when(j > me)
                def _():
                    part_send[h, j, :ROWS, :] = part
                    part_send[h, j, ROWS:, :] = stat_part
                    p_copy(h, j).start()

                @pl.when(j == me)
                def _():
                    part_recv[h, me, :ROWS, :] = part
                    part_recv[h, me, ROWS:, :] = stat_part

    def p_copy(h, j):
        return pltpu.make_async_remote_copy(
            src_ref=part_send.at[h, j],
            dst_ref=part_recv.at[h, me],
            send_sem=p_sent.at[h, j],
            recv_sem=p_came.at[h, me],
            device_id={"ctx": j},
            device_id_type=MESH,
        )

    def out_copies(h):
        for part in range(2):
            columns = pl.ds(pl.multiple_of((part * KVH + h) * HD, HD), HD)
            yield pltpu.make_async_copy(
                context.at[:, columns], context_out.at[:, columns], out_done.at[h, part]
            )

    def assemble(h):
        @pl.loop(1, owner_count)
        def _(step):
            source = lax.rem(me_o + step, owner_count)
            stage[pl.ds(source * CAP, CAP)] = x_recv[h, source]

        stage[pl.ds(me_o * CAP, CAP)] = own[h, : CAP * BLK].reshape(CAP, BLK, 2 * HD)
        fresh_rows = fresh[h]
        for b in range(NBD):
            rows = slice(b * BLK, (b + 1) * BLK)
            match = (
                lax.broadcasted_iota(jnp.int32, (BLK, BLK), 0) + b * BLK == place_row
            ).astype(f32)
            replaced = jnp.sum(match, axis=1, keepdims=True) > 0.5
            placed = jnp.dot(match.astype(bf16), fresh_rows, preferred_element_type=f32)
            block = stage[where_from[b]].astype(f32)
            block = jnp.where(usable[b], block, 0.0)
            block = jnp.where(replaced, placed, block).astype(bf16)
            context[rows, pl.ds(pl.multiple_of(h * HD, HD), HD)] = block[:, :HD]
            context[rows, pl.ds(pl.multiple_of((KVH + h) * HD, HD), HD)] = block[:, HD:]
        for copy in out_copies(h):
            copy.start()

    def combine(h):
        @pl.loop(0, me)
        def _(source):
            pltpu.make_async_remote_copy(
                src_ref=part_send.at[h, source],
                dst_ref=part_recv.at[h, source],
                send_sem=p_sent.at[h, source],
                recv_sem=p_came.at[h, source],
                device_id={"ctx": source},
                device_id_type=MESH,
            ).wait_recv()

        for c in range(cycle_size):
            pieces = part_recv[h, c, ROWS:, :].astype(f32)
            level = jnp.sum(pieces, axis=0, keepdims=True)
            levels[c : c + 1, :] = jnp.where(c <= me, level, 2 * HIDDEN)
        level = levels[...]
        share = jnp.exp2(level - jnp.max(level, axis=0, keepdims=True))
        share = share / jnp.sum(share, axis=0, keepdims=True)
        if cycle_size < BLK:
            share = jnp.concatenate(
                [share, jnp.zeros((BLK - cycle_size, BLK), f32)], axis=0
            )
        shares[...] = share.T
        mine = shares[pl.ds(lax.rem(me, 2) * ROWS, ROWS), :]
        result = jnp.zeros((ROWS, HD), f32)
        for c in range(cycle_size):
            part = jnp.where(c <= me, part_recv[h, c, :ROWS, :].astype(f32), 0.0)
            result = result + part * mine[:, c : c + 1]
        attended[h] = result.astype(bf16)

    attend_own(0)
    attend_own(1)
    attend_others(0)

    @pl.loop(1, KVH)
    def _(h):
        @pl.when(h < KVH - 1)
        def _():
            attend_own(h + 1)

        assemble(h - 1)
        attend_others(h)
        combine(h - 1)

    assemble(KVH - 1)
    combine(KVH - 1)

    for h in range(KVH):
        x_wait_send(h)

    @pl.loop(0, KVH)
    def _(h):
        for copy in out_copies(h):
            copy.wait()

        @pl.loop(0, me)
        def _(peer):
            q_copy(h, peer).wait_send()

        @pl.loop(me + 1, cycle_size)
        def _(j):
            p_copy(h, j).wait_send()

    @pl.loop(1, cycle_size)
    def _(step):
        r_copy(lax.rem(me + step, cycle_size)).wait_send()


def on_device(span_cache, retrieval, counts, recompute_pos, hidden, kv_weight, queries, block_mask):
    owner_count = lax.axis_size("owner")
    cycle_size = lax.axis_size("ctx")
    width = span_cache.shape[2]
    bf16, f32 = jnp.bfloat16, jnp.float32
    grouped = queries[0].reshape(RCP, KVH, GROUP, HD).transpose(1, 2, 0, 3)
    grouped = grouped.reshape(KVH, ROWS, HD)
    vmem = pl.BlockSpec(memory_space=pltpu.VMEM)
    smem = pl.BlockSpec(memory_space=pltpu.SMEM)
    dma = pltpu.SemaphoreType.DMA
    context, attended = pl.pallas_call(
        functools.partial(kernel, owner_count, cycle_size),
        out_shape=(
            jax.ShapeDtypeStruct((CTX_DEV, width), bf16),
            jax.ShapeDtypeStruct((KVH, ROWS, HD), bf16),
        ),
        in_specs=[smem] * 3 + [vmem] * 6,
        out_specs=(pl.BlockSpec(memory_space=pl.ANY), vmem),
        scratch_shapes=[
            pltpu.VMEM((KVH, owner_count, CAP, BLK, 2 * HD), bf16),
            pltpu.VMEM((KVH, owner_count, CAP, BLK, 2 * HD), bf16),
            pltpu.VMEM((KVH, CAP * BLK + BLK, 2 * HD), bf16),
            pltpu.VMEM((HD, CAP * BLK + BLK), bf16),
            pltpu.VMEM((owner_count, HD, CAP * BLK), bf16),
            pltpu.VMEM((owner_count * CAP, BLK, 2 * HD), bf16),
            pltpu.VMEM((CTX_DEV, width), bf16),
            pltpu.VMEM((KVH, cycle_size, ROWS, HD), bf16),
            pltpu.VMEM((cycle_size, 2 * RCP, KVH * HD), bf16),
            pltpu.VMEM((cycle_size, 2 * RCP, KVH * HD), bf16),
            pltpu.VMEM((KVH, BLK, 2 * HD), bf16),
            pltpu.VMEM((owner_count, cycle_size * RCP, CAP * BLK + BLK), f32),
            pltpu.VMEM((KVH, cycle_size * ROWS, HD), f32),
            pltpu.VMEM((KVH, cycle_size * ROWS, HD), f32),
            pltpu.VMEM((KVH, cycle_size * ROWS, HD), f32),
            pltpu.VMEM((KVH, cycle_size, ROWS + STAT, HD), bf16),
            pltpu.VMEM((KVH, cycle_size, ROWS + STAT, HD), bf16),
            pltpu.VMEM((cycle_size, BLK), f32),
            pltpu.VMEM((BLK, BLK), f32),
            dma((KVH, owner_count)),
            dma((KVH, owner_count)),
            dma((KVH, cycle_size)),
            dma((KVH, cycle_size)),
            dma((cycle_size,)),
            dma((cycle_size,)),
            dma((KVH, cycle_size)),
            dma((KVH, cycle_size)),
            dma((KVH, 2)),
        ],
        compiler_params=pltpu.CompilerParams(
            collective_id=0, has_side_effects=True, vmem_limit_bytes=56 * 1024 * 1024
        ),
        name="span_attention",
    )(
        retrieval,
        counts,
        recompute_pos,
        recompute_pos,
        block_mask[0].T,
        hidden[0],
        kv_weight,
        grouped,
        span_cache,
    )
    attended = attended.reshape(KVH, GROUP, RCP, HD).transpose(2, 0, 1, 3)
    return (context[None], attended.reshape(1, RCP, QH * HD))


def solution(mesh):
    in_specs = (
        P(("owner", "ctx"), None, None),
        P(None, "ctx"),
        P(),
        P("owner", None),
        P("owner", None, "ctx"),
        P("ctx", None),
        P("owner", "ctx", None),
        P("owner", None, "ctx"),
    )
    out_specs = (P("owner", "ctx", None), P("owner", "ctx", None))
    return jax.shard_map(
        on_device, mesh=mesh, in_specs=in_specs, out_specs=out_specs, check_vma=False
    )
```

```python
import functools

import jax
import jax.numpy as jnp
from jax import lax
from jax.experimental import pallas as pl
from jax.experimental.pallas import tpu as pltpu
from jax.sharding import PartitionSpec as P

QH = 32
KVH = 4
HD = 128
BLK = 128
NBD = 8
RCP = 8
SLOTS = 8
CAP = 4
CTX_DEV = 1024
GROUP = QH // KVH
ROWS = GROUP * RCP
TILE = 4
STAT = 16
HIDDEN = -1e30
LOG2E = 1.4426950408889634
FACTOR = HD ** (-0.5) * LOG2E
MESH = pl.DeviceIdType.MESH


def kernel(
    owner_count,
    cycle_size,
    retrieval,
    counts,
    positions,
    position_row,
    mask_rows,
    hidden,
    weight,
    queries,
    spans,
    context_out,
    attended,
    x_send,
    slots,
    stage,
    context,
    every_query,
    red_send,
    red_recv,
    fresh,
    bias,
    values_ones,
    part_send,
    part_recv,
    levels,
    shares,
    x_sent,
    x_came,
    q_sent,
    q_came,
    r_sent,
    r_came,
    p_sent,
    p_came,
    f_sent,
    out_done,
):
    me_o = lax.axis_index("owner")
    me = lax.axis_index("ctx")
    group_size = cycle_size * SLOTS
    f32, bf16 = jnp.float32, jnp.bfloat16

    barrier = pltpu.get_barrier_semaphore()

    @pl.loop(1, cycle_size)
    def _(step):
        peer = lax.rem(me + step, cycle_size)
        pl.semaphore_signal(barrier, inc=1, device_id={"ctx": peer}, device_id_type=MESH)

    @pl.loop(1, owner_count)
    def _(step):
        peer = lax.rem(me_o + step, owner_count)
        pl.semaphore_signal(barrier, inc=1, device_id={"owner": peer}, device_id_type=MESH)

    def chosen_slots(request):
        count = counts[request]
        rank = jnp.int32(0)
        chosen = [jnp.int32(0)] * CAP
        for b in range(NBD):
            span = retrieval[request, b]
            mine = (me * NBD + b < count) & (lax.div(span, group_size) == me_o)
            for k in range(CAP):
                chosen[k] = jnp.where(mine & (rank == k), lax.rem(span, SLOTS), chosen[k])
            rank = rank + jnp.where(mine, 1, 0)
        return chosen

    def pack(request, store):
        chosen = chosen_slots(request)
        for h in range(KVH):
            for k in range(CAP):
                for part in range(2):
                    column = (part * KVH + h) * HD
                    store(h, k, part, spans[chosen[k], :, column : column + HD])

    def x_copy(h, step):
        peer = lax.rem(me_o + step, owner_count)
        return pltpu.make_async_remote_copy(
            src_ref=x_send.at[h, peer],
            dst_ref=slots.at[h, pl.ds(me_o * CAP, CAP)],
            send_sem=x_sent.at[h, peer],
            recv_sem=x_came.at[h, me_o],
            device_id={"owner": peer},
            device_id_type=MESH,
        )

    @pl.loop(1, owner_count)
    def _(step):
        peer = lax.rem(me_o + step, owner_count)

        def store(h, k, part, block):
            x_send[h, peer, k, :, part * HD : (part + 1) * HD] = block

        pack(peer, store)

    pl.semaphore_wait(barrier, cycle_size + owner_count - 2)

    for h in range(KVH):

        @pl.loop(1, owner_count)
        def _(step):
            x_copy(h, step).start()

    def q_copy(h, peer):
        return pltpu.make_async_remote_copy(
            src_ref=queries.at[h],
            dst_ref=every_query.at[h, me],
            send_sem=q_sent.at[h, peer],
            recv_sem=q_came.at[h, me],
            device_id={"ctx": peer},
            device_id_type=MESH,
        )

    my_core = lax.rem(me, 2)
    my_chip = lax.div(me, 2)
    sibling = me + 1 - 2 * my_core

    def q_start(h):
        @pl.when(my_core == 1)
        def _():
            q_copy(h, sibling).start()

        @pl.loop(0, my_chip)
        def _(step):
            q_copy(h, 2 * (my_chip - 1 - step) + my_core).start()

    def forward(h, source):
        return pltpu.make_async_remote_copy(
            src_ref=every_query.at[h, source],
            dst_ref=every_query.at[h, source],
            send_sem=f_sent.at[h, source],
            recv_sem=q_came.at[h, source],
            device_id={"ctx": sibling},
            device_id_type=MESH,
        )

    q_start(0)

    partial = jnp.dot(hidden[...], weight[...], preferred_element_type=f32)
    half = KVH * HD
    for j in range(cycle_size):
        rows = partial[j * RCP : (j + 1) * RCP]
        red_send[j] = jnp.concatenate([rows[:, :half], rows[:, half:]], axis=0).astype(bf16)

    def r_copy(peer):
        return pltpu.make_async_remote_copy(
            src_ref=red_send.at[peer],
            dst_ref=red_recv.at[me],
            send_sem=r_sent.at[peer],
            recv_sem=r_came.at[me],
            device_id={"ctx": peer},
            device_id_type=MESH,
        )

    @pl.loop(1, cycle_size)
    def _(step):
        r_copy(lax.rem(me + step, cycle_size)).start()

    red_recv[me] = red_send[me]

    for h in range(1, KVH):
        q_start(h)

    for h in range(KVH):
        every_query[h, me] = queries[h]

    def store_own(h, k, part, block):
        slots[h, me_o * CAP + k, :, part * HD : (part + 1) * HD] = block

    pack(me_o, store_own)

    my_count = counts[me_o]
    query_total = cycle_size * RCP
    block_total = mask_rows.shape[1]
    index_of = lax.broadcasted_iota(jnp.int32, (1, query_total), 1) // RCP
    own_place = position_row[...]
    query_pos = index_of * CTX_DEV + own_place
    query_block = index_of * NBD + own_place // BLK
    onehot = (
        lax.broadcasted_iota(jnp.int32, (block_total, query_total), 0) == query_block
    ).astype(f32).astype(bf16)
    allowed = jnp.dot(
        mask_rows[...].astype(f32).astype(bf16), onehot, preferred_element_type=f32
    )
    block_row = lax.broadcasted_iota(jnp.int32, (NBD, query_total), 0) + me * NBD
    reach = jnp.where(
        (allowed > 0.5) & (block_row < my_count),
        (query_pos - block_row * BLK).astype(f32),
        -1.0,
    )
    if query_total > NBD:
        reach = jnp.concatenate(
            [reach, jnp.zeros((query_total - NBD, query_total), f32)], axis=0
        )
    reach = reach.T
    lane = lax.broadcasted_iota(jnp.int32, (1, BLK), 1).astype(f32)
    for b in range(NBD):
        bias[:, b * BLK : (b + 1) * BLK] = jnp.where(lane <= reach[:, b : b + 1], 0.0, HIDDEN)

    values_ones[:, HD:] = jnp.ones((CTX_DEV, HD), bf16)

    @pl.loop(1, cycle_size)
    def _(step):
        source = lax.rem(me + step, cycle_size)
        pltpu.make_async_remote_copy(
            src_ref=red_send.at[source],
            dst_ref=red_recv.at[source],
            send_sem=r_sent.at[source],
            recv_sem=r_came.at[source],
            device_id={"ctx": source},
            device_id_type=MESH,
        ).wait_recv()

    total = red_recv[0].astype(f32)
    for c in range(1, cycle_size):
        total = total + red_recv[c].astype(f32)
    fresh[...] = jnp.zeros((KVH, BLK, 2 * HD), bf16)
    for h in range(KVH):
        columns = slice(h * HD, (h + 1) * HD)
        rows = jnp.concatenate([total[:RCP, columns], total[RCP:, columns]], axis=1)
        fresh[h, : 2 * RCP] = jnp.concatenate([rows, jnp.zeros_like(rows)], axis=0).astype(bf16)

    place_lane = lax.broadcasted_iota(jnp.int32, (1, BLK), 1)
    place_row = jnp.full((1, BLK), -1, jnp.int32)
    for i in range(RCP):
        place_row = jnp.where(place_lane == i, positions[0, me * RCP + i], place_row)

    where_from = []
    for b in range(NBD):
        source = lax.div(retrieval[me_o, b], group_size)
        ordinal = jnp.int32(0)
        for a in range(b):
            same = (lax.div(retrieval[me_o, a], group_size) == source) & (
                me * NBD + a < my_count
            )
            ordinal = ordinal + jnp.where(same, 1, 0)
        where_from.append(source * CAP + jnp.minimum(ordinal, CAP - 1))

    def combine(h):
        @pl.loop(0, me)
        def _(source):
            pltpu.make_async_remote_copy(
                src_ref=part_send.at[h, source],
                dst_ref=part_recv.at[h, source],
                send_sem=p_sent.at[h, source],
                recv_sem=p_came.at[h, source],
                device_id={"ctx": source},
                device_id_type=MESH,
            ).wait_recv()

        for c in range(cycle_size):
            pieces = part_recv[h, c, ROWS:, :].astype(f32)
            level = jnp.sum(pieces, axis=0, keepdims=True)
            levels[c : c + 1, :] = jnp.where(c <= me, level, 2 * HIDDEN)
        level = levels[...]
        share = jnp.exp2(level - jnp.max(level, axis=0, keepdims=True))
        share = share / jnp.sum(share, axis=0, keepdims=True)
        if cycle_size < BLK:
            share = jnp.concatenate(
                [share, jnp.zeros((BLK - cycle_size, BLK), f32)], axis=0
            )
        shares[...] = share.T
        mine = shares[pl.ds(lax.rem(me, 2) * ROWS, ROWS), :]
        result = jnp.zeros((ROWS, HD), f32)
        for c in range(cycle_size):
            part = jnp.where(c <= me, part_recv[h, c, :ROWS, :].astype(f32), 0.0)
            result = result + part * mine[:, c : c + 1]
        attended[h] = result.astype(bf16)

    def out_copies(h):
        for part in range(2):
            columns = pl.ds(pl.multiple_of((part * KVH + h) * HD, HD), HD)
            yield pltpu.make_async_copy(
                context.at[:, columns], context_out.at[:, columns], out_done.at[h, part]
            )

    def collect(h):
        @pl.loop(my_chip + 1, cycle_size // 2)
        def _(chip):
            arrived = forward(h, 2 * chip + my_core)
            arrived.wait_recv()
            arrived.start()

    @pl.loop(0, KVH)
    def _(h):
        @pl.loop(1, owner_count)
        def _(step):
            source = lax.rem(me_o + step, owner_count)
            pltpu.make_async_remote_copy(
                src_ref=x_send.at[h, source],
                dst_ref=slots.at[h, pl.ds(source * CAP, CAP)],
                send_sem=x_sent.at[h, source],
                recv_sem=x_came.at[h, source],
                device_id={"owner": source},
                device_id_type=MESH,
            ).wait_recv()

        key_columns = pl.ds(pl.multiple_of(h * HD, HD), HD)
        value_columns = pl.ds(pl.multiple_of((KVH + h) * HD, HD), HD)
        fresh_rows = fresh[h]
        stage[...] = slots[h]
        for b in range(NBD):
            rows = slice(b * BLK, (b + 1) * BLK)
            match = (
                lax.broadcasted_iota(jnp.int32, (BLK, BLK), 0) + b * BLK == place_row
            ).astype(f32)
            replaced = jnp.sum(match, axis=1, keepdims=True) > 0.5
            placed = jnp.dot(match.astype(bf16), fresh_rows, preferred_element_type=f32)
            block = stage[where_from[b]].astype(f32)
            block = jnp.where(me * NBD + b < my_count, block, 0.0)
            block = jnp.where(replaced, placed, block).astype(bf16)
            context[rows, key_columns] = block[:, :HD]
            context[rows, value_columns] = block[:, HD:]
            values_ones[rows, :HD] = block[:, HD:]

        @pl.when(h == 0)
        def _():
            collect(h)

        @pl.loop(my_chip + 1, cycle_size // 2)
        def _(chip):
            forward(h, 2 * chip + 1 - my_core).wait_recv()

        @pl.when(my_core == 0)
        def _():
            forward(h, sibling).wait_recv()

        @pl.loop(lax.div(me, TILE), cycle_size // TILE)
        def _(tile):
            query_rows = every_query[h, pl.ds(tile * TILE, TILE)].reshape(TILE * ROWS, HD)
            scores = lax.dot_general(
                query_rows,
                context[:, key_columns],
                (((1,), (1,)), ((), ())),
                preferred_element_type=f32,
            )
            shift = bias[pl.ds(pl.multiple_of(tile * TILE * RCP, TILE * RCP), TILE * RCP), :]
            scores = scores.reshape(TILE, GROUP, RCP, CTX_DEV) + shift.reshape(
                TILE, 1, RCP, CTX_DEV
            )
            scores = scores.reshape(TILE * ROWS, CTX_DEV)
            highest = jnp.max(scores, axis=1, keepdims=True)
            weights = jnp.exp2((scores - highest) * FACTOR).astype(bf16)
            summed = jnp.dot(weights, values_ones[...], preferred_element_type=f32)
            weight_sum = summed[:, HD:]
            outcome = (summed[:, :HD] / weight_sum).astype(bf16)
            level = highest * FACTOR + jnp.log(weight_sum) * LOG2E
            level = level.T[:STAT]
            high = level.astype(bf16).astype(f32)
            middle = (level - high).astype(bf16).astype(f32)
            low = level - high - middle
            row = lax.broadcasted_iota(jnp.int32, level.shape, 0)
            stat = jnp.where(
                row == 0, high, jnp.where(row == 1, middle, jnp.where(row == 2, low, 0.0))
            ).astype(bf16)
            for jj in range(TILE):
                j = tile * TILE + jj
                pair = jj // 2
                part = outcome[jj * ROWS : (jj + 1) * ROWS]
                stat_part = stat[:, pair * BLK : (pair + 1) * BLK]

                @pl.when(j > me)
                def _():
                    part_send[h, j, :ROWS, :] = part
                    part_send[h, j, ROWS:, :] = stat_part
                    pltpu.make_async_remote_copy(
                        src_ref=part_send.at[h, j],
                        dst_ref=part_recv.at[h, me],
                        send_sem=p_sent.at[h, j],
                        recv_sem=p_came.at[h, me],
                        device_id={"ctx": j},
                        device_id_type=MESH,
                    ).start()

                @pl.when(j == me)
                def _():
                    part_recv[h, me, :ROWS, :] = part
                    part_recv[h, me, ROWS:, :] = stat_part

        for copy in out_copies(h):
            copy.start()

        @pl.when(h < KVH - 1)
        def _():
            collect(h + 1)

        @pl.when(h > 0)
        def _():
            combine(h - 1)

    combine(KVH - 1)

    @pl.loop(0, KVH)
    def _(h):
        @pl.loop(1, owner_count)
        def _(step):
            x_copy(h, step).wait_send()

        for copy in out_copies(h):
            copy.wait()

        @pl.when(my_core == 1)
        def _():
            q_copy(h, sibling).wait_send()

        @pl.loop(0, my_chip)
        def _(step):
            q_copy(h, 2 * (my_chip - 1 - step) + my_core).wait_send()

        @pl.loop(my_chip + 1, cycle_size // 2)
        def _(chip):
            forward(h, 2 * chip + my_core).wait_send()

        @pl.loop(me + 1, cycle_size)
        def _(j):
            pltpu.make_async_remote_copy(
                src_ref=part_send.at[h, j],
                dst_ref=part_recv.at[h, me],
                send_sem=p_sent.at[h, j],
                recv_sem=p_came.at[h, me],
                device_id={"ctx": j},
                device_id_type=MESH,
            ).wait_send()

    @pl.loop(1, cycle_size)
    def _(step):
        r_copy(lax.rem(me + step, cycle_size)).wait_send()


def on_device(span_cache, retrieval, counts, recompute_pos, hidden, kv_weight, queries, block_mask):
    owner_count = lax.axis_size("owner")
    cycle_size = lax.axis_size("ctx")
    width = span_cache.shape[2]
    bf16 = jnp.bfloat16
    grouped = queries[0].reshape(RCP, KVH, GROUP, HD).transpose(1, 2, 0, 3)
    grouped = grouped.reshape(KVH, ROWS, HD)
    vmem = pl.BlockSpec(memory_space=pltpu.VMEM)
    smem = pl.BlockSpec(memory_space=pltpu.SMEM)
    dma = pltpu.SemaphoreType.DMA
    context, attended = pl.pallas_call(
        functools.partial(kernel, owner_count, cycle_size),
        out_shape=(
            jax.ShapeDtypeStruct((CTX_DEV, width), bf16),
            jax.ShapeDtypeStruct((KVH, ROWS, HD), bf16),
        ),
        in_specs=[smem] * 3 + [vmem] * 6,
        out_specs=(pl.BlockSpec(memory_space=pl.ANY), vmem),
        scratch_shapes=[
            pltpu.VMEM((KVH, owner_count, CAP, BLK, 2 * HD), bf16),
            pltpu.VMEM((KVH, owner_count * CAP, BLK, 2 * HD), bf16),
            pltpu.VMEM((owner_count * CAP, BLK, 2 * HD), bf16),
            pltpu.VMEM((CTX_DEV, width), bf16),
            pltpu.VMEM((KVH, cycle_size, ROWS, HD), bf16),
            pltpu.VMEM((cycle_size, 2 * RCP, KVH * HD), bf16),
            pltpu.VMEM((cycle_size, 2 * RCP, KVH * HD), bf16),
            pltpu.VMEM((KVH, BLK, 2 * HD), bf16),
            pltpu.VMEM((cycle_size * RCP, CTX_DEV), jnp.float32),
            pltpu.VMEM((CTX_DEV, 2 * HD), bf16),
            pltpu.VMEM((KVH, cycle_size, ROWS + STAT, HD), bf16),
            pltpu.VMEM((KVH, cycle_size, ROWS + STAT, HD), bf16),
            pltpu.VMEM((cycle_size, BLK), jnp.float32),
            pltpu.VMEM((BLK, BLK), jnp.float32),
            dma((KVH, owner_count)),
            dma((KVH, owner_count)),
            dma((KVH, cycle_size)),
            dma((KVH, cycle_size)),
            dma((cycle_size,)),
            dma((cycle_size,)),
            dma((KVH, cycle_size)),
            dma((KVH, cycle_size)),
            dma((KVH, cycle_size)),
            dma((KVH, 2)),
        ],
        compiler_params=pltpu.CompilerParams(
            collective_id=0, has_side_effects=True, vmem_limit_bytes=56 * 1024 * 1024
        ),
        name="span_attention",
    )(
        retrieval,
        counts,
        recompute_pos,
        recompute_pos,
        block_mask[0].T,
        hidden[0],
        kv_weight,
        grouped,
        span_cache,
    )
    attended = attended.reshape(KVH, GROUP, RCP, HD).transpose(2, 0, 1, 3)
    return (context[None], attended.reshape(1, RCP, QH * HD))


def solution(mesh):
    in_specs = (
        P(("owner", "ctx"), None, None),
        P(None, "ctx"),
        P(),
        P("owner", None),
        P("owner", None, "ctx"),
        P("ctx", None),
        P("owner", "ctx", None),
        P("owner", None, "ctx"),
    )
    out_specs = (P("owner", "ctx", None), P("owner", "ctx", None))
    return jax.shard_map(
        on_device, mesh=mesh, in_specs=in_specs, out_specs=out_specs, check_vma=False
    )
```

```python
import functools

import jax
import jax.numpy as jnp
from jax import lax
from jax.experimental import pallas as pl
from jax.experimental.pallas import tpu as pltpu
from jax.sharding import PartitionSpec as P

QH = 32
KVH = 4
HD = 128
BLK = 128
NBD = 8
RCP = 8
SLOTS = 8
CAP = 4
CTX_DEV = 1024
GROUP = QH // KVH
ROWS = GROUP * RCP
TILE = 4
STAT = 16
HIDDEN = -1e30
LOG2E = 1.4426950408889634
FACTOR = HD ** (-0.5) * LOG2E
MESH = pl.DeviceIdType.MESH


def kernel(
    owner_count,
    cycle_size,
    retrieval,
    counts,
    positions,
    position_row,
    mask_rows,
    hidden,
    weight,
    queries,
    spans,
    context_out,
    attended,
    x_send,
    slots,
    stage,
    context,
    every_query,
    red_send,
    red_recv,
    fresh,
    bias,
    values_ones,
    part_send,
    part_recv,
    levels,
    shares,
    x_sent,
    x_came,
    q_sent,
    q_came,
    r_sent,
    r_came,
    p_sent,
    p_came,
    f_sent,
    out_done,
):
    me_o = lax.axis_index("owner")
    me = lax.axis_index("ctx")
    group_size = cycle_size * SLOTS
    f32, bf16 = jnp.float32, jnp.bfloat16

    barrier = pltpu.get_barrier_semaphore()

    @pl.loop(1, cycle_size)
    def _(step):
        peer = lax.rem(me + step, cycle_size)
        pl.semaphore_signal(barrier, inc=1, device_id={"ctx": peer}, device_id_type=MESH)

    @pl.loop(1, owner_count)
    def _(step):
        peer = lax.rem(me_o + step, owner_count)
        pl.semaphore_signal(barrier, inc=1, device_id={"owner": peer}, device_id_type=MESH)

    def chosen_slots(request):
        count = counts[request]
        rank = jnp.int32(0)
        chosen = [jnp.int32(0)] * CAP
        for b in range(NBD):
            span = retrieval[request, b]
            mine = (me * NBD + b < count) & (lax.div(span, group_size) == me_o)
            for k in range(CAP):
                chosen[k] = jnp.where(mine & (rank == k), lax.rem(span, SLOTS), chosen[k])
            rank = rank + jnp.where(mine, 1, 0)
        return chosen

    def pack(request, store):
        chosen = chosen_slots(request)
        for h in range(KVH):
            for k in range(CAP):
                for part in range(2):
                    column = (part * KVH + h) * HD
                    store(h, k, part, spans[chosen[k], :, column : column + HD])

    def x_copy(h, step):
        peer = lax.rem(me_o + step, owner_count)
        return pltpu.make_async_remote_copy(
            src_ref=x_send.at[h, peer],
            dst_ref=slots.at[h, pl.ds(me_o * CAP, CAP)],
            send_sem=x_sent.at[h, peer],
            recv_sem=x_came.at[h, me_o],
            device_id={"owner": peer},
            device_id_type=MESH,
        )

    @pl.loop(1, owner_count)
    def _(step):
        peer = lax.rem(me_o + step, owner_count)

        def store(h, k, part, block):
            x_send[h, peer, k, :, part * HD : (part + 1) * HD] = block

        pack(peer, store)

    pl.semaphore_wait(barrier, cycle_size + owner_count - 2)

    for h in range(KVH):

        @pl.loop(1, owner_count)
        def _(step):
            x_copy(h, step).start()

    def q_copy(h, peer):
        return pltpu.make_async_remote_copy(
            src_ref=queries.at[h],
            dst_ref=every_query.at[h, me],
            send_sem=q_sent.at[h, peer],
            recv_sem=q_came.at[h, me],
            device_id={"ctx": peer},
            device_id_type=MESH,
        )

    my_core = lax.rem(me, 2)
    my_chip = lax.div(me, 2)
    sibling = me + 1 - 2 * my_core

    def q_start(h):
        @pl.when(my_core == 1)
        def _():
            q_copy(h, sibling).start()

        @pl.loop(0, my_chip)
        def _(step):
            q_copy(h, 2 * (my_chip - 1 - step) + my_core).start()

    def forward(h, source):
        return pltpu.make_async_remote_copy(
            src_ref=every_query.at[h, source],
            dst_ref=every_query.at[h, source],
            send_sem=f_sent.at[h, source],
            recv_sem=q_came.at[h, source],
            device_id={"ctx": sibling},
            device_id_type=MESH,
        )

    q_start(0)

    partial = jnp.dot(hidden[...], weight[...], preferred_element_type=f32)
    half = KVH * HD
    for j in range(cycle_size):
        rows = partial[j * RCP : (j + 1) * RCP]
        red_send[j] = jnp.concatenate([rows[:, :half], rows[:, half:]], axis=0).astype(bf16)

    def r_copy(peer):
        return pltpu.make_async_remote_copy(
            src_ref=red_send.at[peer],
            dst_ref=red_recv.at[me],
            send_sem=r_sent.at[peer],
            recv_sem=r_came.at[me],
            device_id={"ctx": peer},
            device_id_type=MESH,
        )

    @pl.loop(1, cycle_size)
    def _(step):
        r_copy(lax.rem(me + step, cycle_size)).start()

    red_recv[me] = red_send[me]

    for h in range(1, KVH):
        q_start(h)

    for h in range(KVH):
        every_query[h, me] = queries[h]

    def store_own(h, k, part, block):
        slots[h, me_o * CAP + k, :, part * HD : (part + 1) * HD] = block

    pack(me_o, store_own)

    my_count = counts[me_o]
    query_total = cycle_size * RCP
    block_total = mask_rows.shape[1]
    index_of = lax.broadcasted_iota(jnp.int32, (1, query_total), 1) // RCP
    own_place = position_row[...]
    query_pos = index_of * CTX_DEV + own_place
    query_block = index_of * NBD + own_place // BLK
    onehot = (
        lax.broadcasted_iota(jnp.int32, (block_total, query_total), 0) == query_block
    ).astype(f32).astype(bf16)
    allowed = jnp.dot(
        mask_rows[...].astype(f32).astype(bf16), onehot, preferred_element_type=f32
    )
    block_row = lax.broadcasted_iota(jnp.int32, (NBD, query_total), 0) + me * NBD
    reach = jnp.where(
        (allowed > 0.5) & (block_row < my_count),
        (query_pos - block_row * BLK).astype(f32),
        -1.0,
    )
    if query_total > NBD:
        reach = jnp.concatenate(
            [reach, jnp.zeros((query_total - NBD, query_total), f32)], axis=0
        )
    reach = reach.T
    lane = lax.broadcasted_iota(jnp.int32, (1, BLK), 1).astype(f32)
    for b in range(NBD):
        bias[:, b * BLK : (b + 1) * BLK] = jnp.where(lane <= reach[:, b : b + 1], 0.0, HIDDEN)

    values_ones[:, HD:] = jnp.ones((CTX_DEV, HD), bf16)

    @pl.loop(1, cycle_size)
    def _(step):
        source = lax.rem(me + step, cycle_size)
        pltpu.make_async_remote_copy(
            src_ref=red_send.at[source],
            dst_ref=red_recv.at[source],
            send_sem=r_sent.at[source],
            recv_sem=r_came.at[source],
            device_id={"ctx": source},
            device_id_type=MESH,
        ).wait_recv()

    total = red_recv[0].astype(f32)
    for c in range(1, cycle_size):
        total = total + red_recv[c].astype(f32)
    fresh[...] = jnp.zeros((KVH, BLK, 2 * HD), bf16)
    for h in range(KVH):
        columns = slice(h * HD, (h + 1) * HD)
        rows = jnp.concatenate([total[:RCP, columns], total[RCP:, columns]], axis=1)
        fresh[h, : 2 * RCP] = jnp.concatenate([rows, jnp.zeros_like(rows)], axis=0).astype(bf16)

    place_lane = lax.broadcasted_iota(jnp.int32, (1, BLK), 1)
    place_row = jnp.full((1, BLK), -1, jnp.int32)
    for i in range(RCP):
        place_row = jnp.where(place_lane == i, positions[0, me * RCP + i], place_row)

    where_from = []
    for b in range(NBD):
        source = lax.div(retrieval[me_o, b], group_size)
        ordinal = jnp.int32(0)
        for a in range(b):
            same = (lax.div(retrieval[me_o, a], group_size) == source) & (
                me * NBD + a < my_count
            )
            ordinal = ordinal + jnp.where(same, 1, 0)
        where_from.append(source * CAP + jnp.minimum(ordinal, CAP - 1))

    def combine(h):
        @pl.loop(0, me)
        def _(source):
            pltpu.make_async_remote_copy(
                src_ref=part_send.at[h, source],
                dst_ref=part_recv.at[h, source],
                send_sem=p_sent.at[h, source],
                recv_sem=p_came.at[h, source],
                device_id={"ctx": source},
                device_id_type=MESH,
            ).wait_recv()

        for c in range(cycle_size):
            pieces = part_recv[h, c, ROWS:, :].astype(f32)
            level = jnp.sum(pieces, axis=0, keepdims=True)
            levels[c : c + 1, :] = jnp.where(c <= me, level, 2 * HIDDEN)
        level = levels[...]
        share = jnp.exp2(level - jnp.max(level, axis=0, keepdims=True))
        share = share / jnp.sum(share, axis=0, keepdims=True)
        if cycle_size < BLK:
            share = jnp.concatenate(
                [share, jnp.zeros((BLK - cycle_size, BLK), f32)], axis=0
            )
        shares[...] = share.T
        mine = shares[pl.ds(lax.rem(me, 2) * ROWS, ROWS), :]
        result = jnp.zeros((ROWS, HD), f32)
        for c in range(cycle_size):
            part = jnp.where(c <= me, part_recv[h, c, :ROWS, :].astype(f32), 0.0)
            result = result + part * mine[:, c : c + 1]
        attended[h] = result.astype(bf16)

    def out_copies(h):
        for part in range(2):
            columns = pl.ds(pl.multiple_of((part * KVH + h) * HD, HD), HD)
            yield pltpu.make_async_copy(
                context.at[:, columns], context_out.at[:, columns], out_done.at[h, part]
            )

    def collect(h):
        @pl.loop(my_chip + 1, cycle_size // 2)
        def _(chip):
            arrived = forward(h, 2 * chip + my_core)
            arrived.wait_recv()
            arrived.start()

    @pl.loop(0, KVH)
    def _(h):
        @pl.loop(1, owner_count)
        def _(step):
            source = lax.rem(me_o + step, owner_count)
            pltpu.make_async_remote_copy(
                src_ref=x_send.at[h, source],
                dst_ref=slots.at[h, pl.ds(source * CAP, CAP)],
                send_sem=x_sent.at[h, source],
                recv_sem=x_came.at[h, source],
                device_id={"owner": source},
                device_id_type=MESH,
            ).wait_recv()

        key_columns = pl.ds(pl.multiple_of(h * HD, HD), HD)
        value_columns = pl.ds(pl.multiple_of((KVH + h) * HD, HD), HD)
        fresh_rows = fresh[h]
        stage[...] = slots[h]
        for b in range(NBD):
            rows = slice(b * BLK, (b + 1) * BLK)
            match = (
                lax.broadcasted_iota(jnp.int32, (BLK, BLK), 0) + b * BLK == place_row
            ).astype(f32)
            replaced = jnp.sum(match, axis=1, keepdims=True) > 0.5
            placed = jnp.dot(match.astype(bf16), fresh_rows, preferred_element_type=f32)
            block = stage[where_from[b]].astype(f32)
            block = jnp.where(me * NBD + b < my_count, block, 0.0)
            block = jnp.where(replaced, placed, block).astype(bf16)
            context[rows, key_columns] = block[:, :HD]
            context[rows, value_columns] = block[:, HD:]
            values_ones[rows, :HD] = block[:, HD:]

        @pl.when(h == 0)
        def _():
            collect(h)

        @pl.loop(my_chip + 1, cycle_size // 2)
        def _(chip):
            forward(h, 2 * chip + 1 - my_core).wait_recv()

        @pl.when(my_core == 0)
        def _():
            forward(h, sibling).wait_recv()

        @pl.loop(0, cycle_size // TILE - lax.div(me, TILE))
        def _(step):
            tile = cycle_size // TILE - 1 - step
            query_rows = every_query[h, pl.ds(tile * TILE, TILE)].reshape(TILE * ROWS, HD)
            scores = lax.dot_general(
                query_rows,
                context[:, key_columns],
                (((1,), (1,)), ((), ())),
                preferred_element_type=f32,
            )
            shift = bias[pl.ds(pl.multiple_of(tile * TILE * RCP, TILE * RCP), TILE * RCP), :]
            scores = scores.reshape(TILE, GROUP, RCP, CTX_DEV) + shift.reshape(
                TILE, 1, RCP, CTX_DEV
            )
            scores = scores.reshape(TILE * ROWS, CTX_DEV)
            highest = jnp.max(scores, axis=1, keepdims=True)
            weights = jnp.exp2((scores - highest) * FACTOR).astype(bf16)
            summed = jnp.dot(weights, values_ones[...], preferred_element_type=f32)
            weight_sum = summed[:, HD:]
            outcome = (summed[:, :HD] / weight_sum).astype(bf16)
            level = highest * FACTOR + jnp.log(weight_sum) * LOG2E
            level = level.T[:STAT]
            high = level.astype(bf16).astype(f32)
            middle = (level - high).astype(bf16).astype(f32)
            low = level - high - middle
            row = lax.broadcasted_iota(jnp.int32, level.shape, 0)
            stat = jnp.where(
                row == 0, high, jnp.where(row == 1, middle, jnp.where(row == 2, low, 0.0))
            ).astype(bf16)
            for jj in reversed(range(TILE)):
                j = tile * TILE + jj
                pair = jj // 2
                part = outcome[jj * ROWS : (jj + 1) * ROWS]
                stat_part = stat[:, pair * BLK : (pair + 1) * BLK]

                @pl.when(j > me)
                def _():
                    part_send[h, j, :ROWS, :] = part
                    part_send[h, j, ROWS:, :] = stat_part
                    pltpu.make_async_remote_copy(
                        src_ref=part_send.at[h, j],
                        dst_ref=part_recv.at[h, me],
                        send_sem=p_sent.at[h, j],
                        recv_sem=p_came.at[h, me],
                        device_id={"ctx": j},
                        device_id_type=MESH,
                    ).start()

                @pl.when(j == me)
                def _():
                    part_recv[h, me, :ROWS, :] = part
                    part_recv[h, me, ROWS:, :] = stat_part

        for copy in out_copies(h):
            copy.start()

        @pl.when(h < KVH - 1)
        def _():
            collect(h + 1)

        @pl.when(h > 0)
        def _():
            combine(h - 1)

    combine(KVH - 1)

    @pl.loop(0, KVH)
    def _(h):
        @pl.loop(1, owner_count)
        def _(step):
            x_copy(h, step).wait_send()

        for copy in out_copies(h):
            copy.wait()

        @pl.when(my_core == 1)
        def _():
            q_copy(h, sibling).wait_send()

        @pl.loop(0, my_chip)
        def _(step):
            q_copy(h, 2 * (my_chip - 1 - step) + my_core).wait_send()

        @pl.loop(my_chip + 1, cycle_size // 2)
        def _(chip):
            forward(h, 2 * chip + my_core).wait_send()

        @pl.loop(me + 1, cycle_size)
        def _(j):
            pltpu.make_async_remote_copy(
                src_ref=part_send.at[h, j],
                dst_ref=part_recv.at[h, me],
                send_sem=p_sent.at[h, j],
                recv_sem=p_came.at[h, me],
                device_id={"ctx": j},
                device_id_type=MESH,
            ).wait_send()

    @pl.loop(1, cycle_size)
    def _(step):
        r_copy(lax.rem(me + step, cycle_size)).wait_send()


def on_device(span_cache, retrieval, counts, recompute_pos, hidden, kv_weight, queries, block_mask):
    owner_count = lax.axis_size("owner")
    cycle_size = lax.axis_size("ctx")
    width = span_cache.shape[2]
    bf16 = jnp.bfloat16
    grouped = queries[0].reshape(RCP, KVH, GROUP, HD).transpose(1, 2, 0, 3)
    grouped = grouped.reshape(KVH, ROWS, HD)
    vmem = pl.BlockSpec(memory_space=pltpu.VMEM)
    smem = pl.BlockSpec(memory_space=pltpu.SMEM)
    dma = pltpu.SemaphoreType.DMA
    context, attended = pl.pallas_call(
        functools.partial(kernel, owner_count, cycle_size),
        out_shape=(
            jax.ShapeDtypeStruct((CTX_DEV, width), bf16),
            jax.ShapeDtypeStruct((KVH, ROWS, HD), bf16),
        ),
        in_specs=[smem] * 3 + [vmem] * 6,
        out_specs=(pl.BlockSpec(memory_space=pl.ANY), vmem),
        scratch_shapes=[
            pltpu.VMEM((KVH, owner_count, CAP, BLK, 2 * HD), bf16),
            pltpu.VMEM((KVH, owner_count * CAP, BLK, 2 * HD), bf16),
            pltpu.VMEM((owner_count * CAP, BLK, 2 * HD), bf16),
            pltpu.VMEM((CTX_DEV, width), bf16),
            pltpu.VMEM((KVH, cycle_size, ROWS, HD), bf16),
            pltpu.VMEM((cycle_size, 2 * RCP, KVH * HD), bf16),
            pltpu.VMEM((cycle_size, 2 * RCP, KVH * HD), bf16),
            pltpu.VMEM((KVH, BLK, 2 * HD), bf16),
            pltpu.VMEM((cycle_size * RCP, CTX_DEV), jnp.float32),
            pltpu.VMEM((CTX_DEV, 2 * HD), bf16),
            pltpu.VMEM((KVH, cycle_size, ROWS + STAT, HD), bf16),
            pltpu.VMEM((KVH, cycle_size, ROWS + STAT, HD), bf16),
            pltpu.VMEM((cycle_size, BLK), jnp.float32),
            pltpu.VMEM((BLK, BLK), jnp.float32),
            dma((KVH, owner_count)),
            dma((KVH, owner_count)),
            dma((KVH, cycle_size)),
            dma((KVH, cycle_size)),
            dma((cycle_size,)),
            dma((cycle_size,)),
            dma((KVH, cycle_size)),
            dma((KVH, cycle_size)),
            dma((KVH, cycle_size)),
            dma((KVH, 2)),
        ],
        compiler_params=pltpu.CompilerParams(
            collective_id=0, has_side_effects=True, vmem_limit_bytes=56 * 1024 * 1024
        ),
        name="span_attention",
    )(
        retrieval,
        counts,
        recompute_pos,
        recompute_pos,
        block_mask[0].T,
        hidden[0],
        kv_weight,
        grouped,
        span_cache,
    )
    attended = attended.reshape(KVH, GROUP, RCP, HD).transpose(2, 0, 1, 3)
    return (context[None], attended.reshape(1, RCP, QH * HD))


def solution(mesh):
    in_specs = (
        P(("owner", "ctx"), None, None),
        P(None, "ctx"),
        P(),
        P("owner", None),
        P("owner", None, "ctx"),
        P("ctx", None),
        P("owner", "ctx", None),
        P("owner", None, "ctx"),
    )
    out_specs = (P("owner", "ctx", None), P("owner", "ctx", None))
    return jax.shard_map(
        on_device, mesh=mesh, in_specs=in_specs, out_specs=out_specs, check_vma=False
    )
```
